128 devices in a mesh: fsdp: 32 (over y, z, core), dp: 4 (over x).
Axes of the slice: x: 4, y: 4, z: 4, core: 2. Of those that a mesh axis runs over, the one named last changes fastest.
Arguments:
- tokens: bfloat16 [4, 512, 6144], P('dp', 'fsdp'), may hold values from -6 to 6
- out_grad: bfloat16 [4, 512, 6144], P('dp', 'fsdp'), may hold values from -6 to 6
- row_prob: float32 [4, 1024], P('dp'), may hold values from 0.1 to 1
- row_token: int32 [4, 1024], P('dp'), may hold values from 0 to 512, as said below
- block_expert: int32 [4, 8], P('dp'), may hold values from 0 to 1, as said below
- w_gate: bfloat16 [2, 6144, 8192], P(None, None, 'fsdp'), may hold values from -0.078125 to 0.078125
- w_up: bfloat16 [2, 6144, 8192], P(None, None, 'fsdp'), may hold values from -0.078125 to 0.078125
- w_down: bfloat16 [2, 8192, 6144], P(None, 'fsdp'), may hold values from -0.0625 to 0.0625
Outputs:
- token_grad: bfloat16 [4, 512, 6144], P('dp', 'fsdp')
- prob_grad: float32 [4, 1024], P('dp')
- gate_grad: bfloat16 [2, 6144, 8192], P(None, 'dp', 'fsdp')
- up_grad: bfloat16 [2, 6144, 8192], P(None, 'dp', 'fsdp')
- down_grad: bfloat16 [2, 8192, 6144], P(None, 'fsdp', 'dp')
The draws below stay inside these ranges and needn't reach their ends.
Inputs may be any that keep to these rules, and one draw needn't show every extreme that they name: `row_token`: in each group the blocks of 128 slots of expert 0 come first, then those of expert 1, then empty blocks. Within an expert's blocks the slots hold the distinct tokens routed to that expert in increasing order, then 512 in the slots left empty. Fewer than 512 tokens are routed to each expert. `block_expert`: never falling along a group; empty blocks carry expert 1.
All inputs are finite; a program needn't handle non-finite values.
Results may differ from the reference program's by a relative error of at most 0.02.
Values may be sent and summed in bfloat16 or wider, within the bound.
A program may use at most 256 MiB of HBM per device.

```python
import jax
import jax.numpy as jnp
from jax import lax

D = 6144
FF = 8192
EXPERTS = 2
BLOCK = 128
GROUPS = 4
GTOK = 512
BLOCKS = 8
ROWS = 1024
HSLICE = 256


def group_topology(group_key):
    first_key, second_key, third_key = jax.random.split(group_key, 3)
    thresholds = jax.random.randint(first_key, (EXPERTS, 1), 35, 96)
    random_rolls = jax.random.randint(second_key, (EXPERTS, GTOK), 0, 100)
    skipped = jax.random.randint(third_key, (EXPERTS, 1), 0, GTOK)
    positions = jnp.arange(GTOK, dtype=jnp.int32)[None, :]
    chosen = ((random_rolls < thresholds) & (positions != skipped)).astype(jnp.int32)
    counts = jnp.sum(chosen, axis=1)
    expert_blocks = (counts + BLOCK - 1) // BLOCK
    block_ends = jnp.cumsum(expert_blocks)
    row_start = (block_ends - expert_blocks) * BLOCK
    slot_index = jnp.cumsum(chosen, axis=1) - 1 + row_start[:, None]
    target = jnp.where(chosen == 1, slot_index, ROWS).astype(jnp.int32)
    token_ids = jnp.broadcast_to(positions, (EXPERTS, GTOK))
    row_token = jnp.full((ROWS,), GTOK, jnp.int32).at[target.reshape(-1)].set(token_ids.reshape(-1), mode='drop')
    block_ids = jnp.arange(BLOCKS, dtype=jnp.int32)
    block_expert = jnp.sum((block_ids[:, None] >= block_ends[None, :-1]).astype(jnp.int32), axis=1)
    return (row_token, block_expert.astype(jnp.int32))


def both_topologies(key):
    group_keys = jax.random.split(key, GROUPS)
    return jax.vmap(group_topology)(group_keys)


def draw_row_token(key, part):
    shared = both_topologies(key)
    return shared[0]


def draw_block_expert(key, part):
    shared = both_topologies(key)
    return shared[1]


def levels(own_key, extent, shards, smallest, high):
    gain, own = 1.0, jax.random.fold_in(own_key, 6)
    for dim, shards_of in shards:
        draws = jnp.exp(jax.random.uniform(jax.random.fold_in(own, dim), (shards_of,), jnp.float32, smallest / len(shards), high / len(shards)))
        gain = gain * jnp.repeat(draws, extent[dim] // shards_of).reshape([-1 if axis == dim else 1 for axis in range(len(extent))])
    return gain


def bell_draw(rng, extent, deviation, bound, cuts=(), held_as=jnp.bfloat16):
    values = jax.random.normal(rng, extent, jnp.float32) * deviation
    if len(cuts) > 0:
        values = levels(rng, extent, cuts, -0.22, 0.18) * values
    return jnp.clip(values, min=-bound, max=bound).astype(held_as)


def setup_inputs(seed: int = 0) -> dict:
    streams_of = jax.random.split(jax.random.key(seed), 9)
    return {
        "tokens": bell_draw(streams_of[0], (GROUPS, GTOK, D), 1.0, 6.0, ((0, 4), (1, 32))),
        "out_grad": bell_draw(streams_of[1], (GROUPS, GTOK, D), 1.0, 6.0, ((0, 4), (1, 32))),
        "row_prob": jnp.clip(0.1 + 0.9 * jax.random.uniform(streams_of[2], (GROUPS, ROWS), jnp.float32) ** levels(streams_of[2], (GROUPS, ROWS), ((0, 4),), -0.2, 0.2), 0.1, 1.0),
        "row_token": draw_row_token(jax.random.fold_in(streams_of[8], 71), 0),
        "block_expert": draw_block_expert(jax.random.fold_in(streams_of[8], 71), 0),
        "w_gate": bell_draw(streams_of[5], (EXPERTS, D, FF), D ** -0.5, 0.078125, ((2, 32),)),
        "w_up": bell_draw(streams_of[6], (EXPERTS, D, FF), D ** -0.5, 0.078125, ((2, 32),)),
        "w_down": bell_draw(streams_of[7], (EXPERTS, FF, D), FF ** -0.5, 0.0625, ((1, 32),)),
    }


def silu_parts(gate_value):
    sigma = jax.nn.sigmoid(gate_value)
    return gate_value * sigma, sigma * (1.0 + gate_value * (1.0 - sigma))


def group_backward(group_tokens, group_grad, group_probs, group_rows, group_experts, w_gate, w_up, w_down):
    zero_row = jnp.zeros((1, D), jnp.bfloat16)
    x_rows = jnp.concatenate([group_tokens, zero_row], 0)[group_rows]
    dy_rows = jnp.concatenate([group_grad, zero_row], 0)[group_rows]
    x_blocks = x_rows.reshape(BLOCKS, BLOCK, D)
    dy_blocks = dy_rows.reshape(BLOCKS, BLOCK, D)
    prob_blocks = group_probs.reshape(BLOCKS, BLOCK)

    def block_terms(inputs):
        x_block, dy_block, prob_block, expert = inputs
        gate_value = jnp.dot(x_block, w_gate[expert], preferred_element_type=jnp.float32)
        up_value = jnp.dot(x_block, w_up[expert], preferred_element_type=jnp.float32)
        silu_value, slope_value = silu_parts(gate_value)
        hidden = lax.optimization_barrier((silu_value * up_value).astype(jnp.bfloat16))
        back = jnp.dot(dy_block, w_down[expert].T, preferred_element_type=jnp.float32)
        prob_part = jnp.sum(hidden.astype(jnp.float32) * back, axis=1)
        scaled = prob_block[:, None] * back
        up_delta = (scaled * silu_value).astype(jnp.bfloat16)
        gate_delta = (scaled * up_value * slope_value).astype(jnp.bfloat16)
        weighted = (prob_block[:, None] * hidden.astype(jnp.float32)).astype(jnp.bfloat16)
        return gate_delta, up_delta, weighted, prob_part

    gate_delta, up_delta, weighted, prob_part = lax.map(block_terms, (x_blocks, dy_blocks, prob_blocks, group_experts))
    prob_grad = prob_part.reshape(ROWS)
    row_blocks = group_rows.reshape(BLOCKS, BLOCK)

    def slice_term(total, slice_index):
        column = slice_index * HSLICE

        def block_term(token_total, inputs):
            gate_block, up_block, expert, block_rows = inputs
            gate_piece = lax.dynamic_slice_in_dim(gate_block, column, HSLICE, 1)
            up_piece = lax.dynamic_slice_in_dim(up_block, column, HSLICE, 1)
            gate_cols = lax.dynamic_slice(w_gate, (expert, jnp.int32(0), column), (1, D, HSLICE))[0]
            up_cols = lax.dynamic_slice(w_up, (expert, jnp.int32(0), column), (1, D, HSLICE))[0]
            rows_term = jnp.dot(gate_piece, gate_cols.T, preferred_element_type=jnp.float32)
            rows_term = rows_term + jnp.dot(up_piece, up_cols.T, preferred_element_type=jnp.float32)
            return token_total.at[block_rows].add(rows_term), None

        token_total, unused = lax.scan(block_term, jnp.zeros((GTOK + 1, D), jnp.float32), (gate_delta, up_delta, group_experts, row_blocks))
        rounded = lax.optimization_barrier(token_total[:GTOK].astype(jnp.bfloat16))
        return total + rounded.astype(jnp.float32), None

    token_sum, unused = lax.scan(slice_term, jnp.zeros((GTOK, D), jnp.float32), jnp.arange(FF // HSLICE, dtype=jnp.int32))

    row_expert = jnp.repeat(group_experts, BLOCK)
    gate_flat = gate_delta.reshape(ROWS, FF)
    up_flat = up_delta.reshape(ROWS, FF)
    weighted_flat = weighted.reshape(ROWS, FF)
    zero_value = jnp.zeros((), jnp.bfloat16)
    gate_list, up_list, down_list = [], [], []
    for expert in range(EXPERTS):
        chosen = (row_expert == expert)[:, None]
        gate_masked = jnp.where(chosen, gate_flat, zero_value)
        up_masked = jnp.where(chosen, up_flat, zero_value)
        weighted_masked = jnp.where(chosen, weighted_flat, zero_value)
        gate_list.append(jnp.dot(x_rows.T, gate_masked, preferred_element_type=jnp.float32).astype(jnp.bfloat16))
        up_list.append(jnp.dot(x_rows.T, up_masked, preferred_element_type=jnp.float32).astype(jnp.bfloat16))
        down_list.append(jnp.dot(weighted_masked.T, dy_rows, preferred_element_type=jnp.float32).astype(jnp.bfloat16))
    return (token_sum.astype(jnp.bfloat16), prob_grad, jnp.stack(gate_list), jnp.stack(up_list), jnp.stack(down_list))


def reference(tokens, out_grad, row_prob, row_token, block_expert, w_gate, w_up, w_down):
    token_list, prob_list = [], []
    gate_total = jnp.zeros((EXPERTS, D, FF), jnp.float32)
    up_total = jnp.zeros((EXPERTS, D, FF), jnp.float32)
    down_total = jnp.zeros((EXPERTS, FF, D), jnp.float32)
    for group_index in range(GROUPS):
        outputs = group_backward(tokens[group_index], out_grad[group_index], row_prob[group_index], row_token[group_index], block_expert[group_index], w_gate, w_up, w_down)
        token_list.append(outputs[0])
        prob_list.append(outputs[1])
        gate_total = gate_total + outputs[2].astype(jnp.float32)
        up_total = up_total + outputs[3].astype(jnp.float32)
        down_total = down_total + outputs[4].astype(jnp.float32)
    return (jnp.stack(token_list), jnp.stack(prob_list), gate_total.astype(jnp.bfloat16), up_total.astype(jnp.bfloat16), down_total.astype(jnp.bfloat16))
```

```python
import jax
import jax.numpy as jnp
from jax import lax
from jax.sharding import PartitionSpec as P

EXPERTS = 2
BLOCK = 128


def silu_parts(gate_value):
    sigma = jax.nn.sigmoid(gate_value)
    return (gate_value * sigma, sigma * (1.0 + gate_value * (1.0 - sigma)))


def dot(a, b, ca, cb):
    return lax.dot_general(a, b, (((ca,), (cb,)), ((), ())), preferred_element_type=jnp.float32)


def shards(tokens, out_grad, row_prob, row_token, block_expert, w_gate, w_up, w_down):
    groups = lax.axis_size("dp")
    local, width = tokens.shape[1:]
    part = width // groups
    hs = w_gate.shape[2]
    x = lax.all_gather(tokens[0], "fsdp", axis=0, tiled=True)
    dy = lax.all_gather(out_grad[0], "fsdp", axis=0, tiled=True)
    gtok = x.shape[0]
    pair = jnp.stack([tokens[0], out_grad[0]]).reshape(2, local, groups, part)
    cols = lax.all_to_all(pair, "dp", split_axis=2, concat_axis=2, tiled=True)
    cols = lax.all_gather(cols, "fsdp", axis=1, tiled=True)
    xc = cols[0].reshape(gtok * groups, part)
    dyc = cols[1].reshape(gtok * groups, part)

    row_expert = jnp.repeat(block_expert[0], BLOCK)
    hit = row_token[0][:, None] == jnp.arange(gtok, dtype=jnp.int32)[None, :]
    deltas, weights, probs = [], [], []
    for e in range(EXPERTS):
        mine = hit & (row_expert == e)[:, None]
        prob = jnp.sum(jnp.where(mine, row_prob[0][:, None], 0.0), axis=0)[:, None]
        gate = dot(x, w_gate[e], 1, 0)
        up = dot(x, w_up[e], 1, 0)
        back = dot(dy, w_down[e], 1, 1)
        silu, slope = silu_parts(gate)
        hidden = (silu * up).astype(jnp.bfloat16).astype(jnp.float32)
        probs.append(jnp.sum(hidden * back, axis=1))
        scaled = prob * back
        deltas.append((scaled * up * slope).astype(jnp.bfloat16))
        deltas.append((scaled * silu).astype(jnp.bfloat16))
        weights.append((prob * hidden).astype(jnp.bfloat16))
    delta = jnp.concatenate(deltas + weights, axis=1)
    everyone = lax.all_gather(delta, "dp", axis=1, tiled=False)
    everyone = everyone.reshape(gtok * groups, delta.shape[1])
    token_part = sum(
        dot(deltas[2 * e + k], w[e], 1, 1)
        for e in range(EXPERTS)
        for k, w in enumerate((w_gate, w_up))
    )
    token_sum = lax.psum_scatter(
        token_part.astype(jnp.bfloat16), "fsdp", scatter_dimension=0, tiled=True
    )
    prob_all = lax.psum(jnp.stack(probs), "fsdp")
    prob_of = jnp.where((row_expert == 0)[:, None], prob_all[0][None], prob_all[1][None])
    prob_sum = jnp.sum(jnp.where(hit, prob_of, 0.0), axis=1)
    gate_grad = jnp.stack(
        [dot(xc, everyone[:, 2 * e * hs : (2 * e + 1) * hs], 0, 0) for e in range(EXPERTS)]
    ).astype(jnp.bfloat16)
    up_grad = jnp.stack(
        [dot(xc, everyone[:, (2 * e + 1) * hs : (2 * e + 2) * hs], 0, 0) for e in range(EXPERTS)]
    ).astype(jnp.bfloat16)
    down_grad = jnp.stack(
        [dot(everyone[:, (4 + e) * hs : (5 + e) * hs], dyc, 0, 0) for e in range(EXPERTS)]
    ).astype(jnp.bfloat16)
    return (token_sum[None], prob_sum[None], gate_grad, up_grad, down_grad)


def solution(mesh):
    in_specs = (
        P("dp", "fsdp", None),
        P("dp", "fsdp", None),
        P("dp", None),
        P("dp", None),
        P("dp", None),
        P(None, None, "fsdp"),
        P(None, None, "fsdp"),
        P(None, "fsdp", None),
    )
    out_specs = (
        P("dp", "fsdp", None),
        P("dp", None),
        P(None, "dp", "fsdp"),
        P(None, "dp", "fsdp"),
        P(None, "fsdp", "dp"),
    )
    return jax.shard_map(shards, mesh=mesh, in_specs=in_specs, out_specs=out_specs, check_vma=False)
```

```python
import functools

import jax
import jax.numpy as jnp
from jax import lax
from jax.experimental import pallas as pl
from jax.experimental.pallas import tpu as pltpu
from jax.sharding import PartitionSpec as P

EXPERTS = 2
BLOCK = 128
SIDE = 4
GROUPS = 4
LOCAL = 16
SLOTS = 32
CHUNK = 128
CHUNK_OF = (0, 1, 3, 2)
BF16 = jnp.bfloat16
F32 = jnp.float32


def dot(a, b, ca, cb):
    return lax.dot_general(a, b, (((ca,), (cb,)), ((), ())), preferred_element_type=F32)


def place():
    f = lax.axis_index("fsdp")
    return f // (2 * SIDE), (f // 2) % SIDE, f % 2


def kernel(
    tokens, out_grad, prob, w_gate, w_up, w_down,
    token_out, prob_out, cols, deltas,
    xs, dys, wg, wu, wd, own, tg, pair_in, half_b, half_a, stage,
    local_sem, send, recv,
):
    y, z, c = place()
    p = lax.axis_index("dp")
    width = xs.shape[1]
    half = width // 2
    part = width // GROUPS
    hs = wg.shape[2]
    count = [0]

    def at(da, db):
        yy = (y + (1 - c) * da + c * db) % SIDE
        zz = (z + c * da + (1 - c) * db) % SIDE
        return {"fsdp": (yy * SIDE + zz) * 2 + c}

    sibling = {"fsdp": (y * SIDE + z) * 2 + 1 - c}

    def over(k):
        return {"dp": (p + k) % GROUPS}

    barrier = pltpu.get_barrier_semaphore()
    peers = [at(1, 0), at(2, 0), at(3, 0), at(0, 1), at(0, 2), at(0, 3), sibling]
    peers += [over(1), over(2), over(3)]
    for peer in peers:
        pl.semaphore_signal(barrier, inc=1, device_id=peer, device_id_type=pl.DeviceIdType.MESH)
    pl.semaphore_wait(barrier, len(peers))

    started = []

    def copy(src, dst, to):
        n = count[0]
        count[0] += 1
        return pltpu.make_async_remote_copy(
            src_ref=src, dst_ref=dst, send_sem=send.at[n], recv_sem=recv.at[n],
            device_id=to, device_id_type=pl.DeviceIdType.MESH,
        )

    def start(one):
        one.start()
        started.append(one)

    def slot_row(i, j):
        return pl.multiple_of(c * (SIDE * LOCAL) + i * LOCAL, LOCAL) + CHUNK_OF[j] * CHUNK

    class Gather:
        def __init__(self, slot, mine, plus):
            far = 3 if plus else 1
            self.slot, self.plus, self.far = slot, plus, far
            self.a = {3: copy(mine, slot(3, 0), at(1, 0)), 1: copy(mine, slot(1, 0), at(3, 0))}
            self.a[2] = copy(slot(far, 0), slot(2, 0), at(1 if plus else 3, 0))
            self.b, self.s = {}, {}
            for i in range(SIDE):
                src = mine if i == 0 else slot(i, 0)
                self.b[i, 3] = copy(src, slot(i, 3), at(0, 1))
                self.b[i, 1] = copy(src, slot(i, 1), at(0, 3))
                self.b[i, 2] = copy(slot(i, far), slot(i, 2), at(0, 1 if plus else 3))
                for j in range(SIDE):
                    src = mine if i == 0 and j == 0 else slot(i, j)
                    self.s[i, j] = copy(src, slot(i, j), sibling)

        def begin_a(self):
            start(self.a[3])
            start(self.a[1])

        def begin_b(self):
            start(self.b[0, 3])
            start(self.b[0, 1])
            start(self.s[0, 0])

        def got_a(self, i):
            self.a[i].wait_recv()
            if i == self.far:
                start(self.a[2])
            start(self.b[i, 3])
            start(self.b[i, 1])
            start(self.s[i, 0])

        def got_b(self, i, j):
            self.b[i, j].wait_recv()
            if j == self.far:
                start(self.b[i, 2])
            start(self.s[i, j])

        def got_s(self, j):
            for i in range(SIDE):
                self.s[i, j].wait_recv()

    row0 = slot_row(0, 0)
    fill = [
        pltpu.make_async_copy(tokens, xs.at[pl.ds(row0, LOCAL)], local_sem.at[0]),
        pltpu.make_async_copy(out_grad, dys.at[pl.ds(row0, LOCAL)], local_sem.at[1]),
        pltpu.make_async_copy(w_gate, wg, local_sem.at[2]),
        pltpu.make_async_copy(w_up, wu, local_sem.at[3]),
        pltpu.make_async_copy(w_down, wd, local_sem.at[4]),
    ]
    ax = Gather(lambda i, j: xs.at[pl.ds(slot_row(i, j), LOCAL)], tokens, True)
    ad = Gather(lambda i, j: dys.at[pl.ds(slot_row(i, j), LOCAL)], out_grad, False)

    def col_slot(k):
        def slot(i, j):
            row = pl.multiple_of(c * (SIDE * LOCAL) + i * LOCAL, LOCAL)
            return cols.at[k, CHUNK_OF[j], pl.ds(1, GROUPS - 1), pl.ds(row, LOCAL)]

        return slot

    bx = Gather(col_slot(0), stage.at[0], True)
    bd = Gather(col_slot(1), stage.at[1], False)

    ax.begin_a()
    ad.begin_a()
    ax.begin_b()
    ad.begin_b()
    swaps = []
    for k, src in enumerate((tokens, out_grad)):
        for step in range(1, GROUPS):
            lane = pl.multiple_of(((p + step) % GROUPS) * part, part)
            swaps.append(
                copy(src.at[:, pl.ds(lane, part)], stage.at[k, GROUPS - step - 1], over(step))
            )
    for one in swaps:
        start(one)
    for one in fill:
        one.start()

    ax.got_a(3)
    ad.got_a(1)
    ax.got_a(1)
    ad.got_a(3)
    ax.got_a(2)
    ad.got_a(2)

    def forward(row, rows):
        where = pl.ds(row, rows)
        for e in range(EXPERTS):
            gate = dot(xs[where], wg[e], 1, 0)
            up = dot(xs[where], wu[e], 1, 0)
            back = dot(dys[where], wd[e], 1, 1)
            sigma = jax.nn.sigmoid(gate)
            silu = gate * sigma
            hidden = (silu * up).astype(BF16).astype(F32)
            prob_out[where, e : e + 1] = jnp.sum(hidden * back, axis=1, keepdims=True)
            share = prob[where, e : e + 1]
            scaled = share * back
            slope = sigma * (1.0 + gate * (1.0 - sigma))
            own[where, 2 * e * hs : (2 * e + 1) * hs] = (scaled * up * slope).astype(BF16)
            own[where, (2 * e + 1) * hs : (2 * e + 2) * hs] = (scaled * silu).astype(BF16)
            own[where, (4 + e) * hs : (5 + e) * hs] = (share * hidden).astype(BF16)

    def token_terms(row, rows):
        where = pl.ds(row, rows)
        step = 512

        def body(n, carry):
            at_n = pl.ds(pl.multiple_of(n * step, step), step)
            total = dot(own[where, 0:hs], wg[0, at_n, :], 1, 1)
            total += dot(own[where, hs : 2 * hs], wu[0, at_n, :], 1, 1)
            total += dot(own[where, 2 * hs : 3 * hs], wg[1, at_n, :], 1, 1)
            total += dot(own[where, 3 * hs : 4 * hs], wu[1, at_n, :], 1, 1)
            tg[where, at_n] = total.astype(BF16)
            return carry

        lax.fori_loop(0, width // step, body, 0)

    ring = {}
    for q in range(SIDE):
        mine = own.at[pl.ds(q * CHUNK, CHUNK)]
        top, bottom = pl.ds(0, CHUNK // 2), pl.ds(CHUNK // 2, CHUNK // 2)
        ring[q] = (
            copy(mine, deltas.at[q, 3], over(1)),
            copy(mine, deltas.at[q, 1], over(3)),
            copy(deltas.at[q, 3, top], deltas.at[q, 2, top], over(1)),
            copy(deltas.at[q, 1, bottom], deltas.at[q, 2, bottom], over(3)),
            pltpu.make_async_copy(mine, deltas.at[q, 0], local_sem.at[5 + q]),
        )
        lane = pl.multiple_of(p * part, part)
        rows = pl.ds(q * CHUNK, CHUNK)
        ring[q] += (
            pltpu.make_async_copy(
                xs.at[rows, pl.ds(lane, part)], cols.at[0, q, 0], local_sem.at[9 + q]
            ),
            pltpu.make_async_copy(
                dys.at[rows, pl.ds(lane, part)], cols.at[1, q, 0], local_sem.at[13 + q]
            ),
        )

    def send_deltas(q):
        start(ring[q][0])
        start(ring[q][1])
        for one in ring[q][4:]:
            one.start()

    def pass_deltas(q):
        ring[q][0].wait_recv()
        start(ring[q][2])
        ring[q][1].wait_recv()
        start(ring[q][3])

    pair = {}
    other = pl.multiple_of((1 - c) * (SIDE * LOCAL), SIDE * LOCAL)
    for q in range(SIDE):
        pair[q] = copy(
            tg.at[pl.ds(q * CHUNK + other, SIDE * LOCAL)], pair_in.at[q], sibling
        )

    for one in fill:
        one.wait()
    ax.got_s(0)
    ad.got_s(0)
    forward(0, CHUNK)
    send_deltas(0)

    for one in swaps:
        one.wait_recv()
    row_c = pl.multiple_of(c * (SIDE * LOCAL), LOCAL)
    bx_own = pltpu.make_async_copy(
        stage.at[0], cols.at[0, 0, pl.ds(1, GROUPS - 1), pl.ds(row_c, LOCAL)], local_sem.at[17]
    )
    bd_own = pltpu.make_async_copy(
        stage.at[1], cols.at[1, 0, pl.ds(1, GROUPS - 1), pl.ds(row_c, LOCAL)], local_sem.at[18]
    )
    bx_own.start()
    bd_own.start()

    for i in (0, 3, 1, 2):
        ax.got_b(i, 3)
        ad.got_b(i, 1)
        ax.got_b(i, 1)
        ad.got_b(i, 3)
    bx.begin_a()
    bd.begin_a()
    bx.begin_b()
    bd.begin_b()
    ax.got_s(1)
    ad.got_s(1)
    ax.got_s(3)
    ad.got_s(3)
    forward(CHUNK, 2 * CHUNK)
    send_deltas(1)
    send_deltas(2)
    pass_deltas(0)

    for i in (0, 3, 1, 2):
        ax.got_b(i, 2)
        ad.got_b(i, 2)
    bx.got_a(3)
    bd.got_a(1)
    bx.got_a(1)
    bd.got_a(3)
    bx.got_a(2)
    bd.got_a(2)
    ax.got_s(2)
    ad.got_s(2)
    forward(3 * CHUNK, CHUNK)
    send_deltas(3)
    token_terms(3 * CHUNK, CHUNK)
    start(pair[3])
    token_terms(0, CHUNK)
    start(pair[0])
    pass_deltas(1)
    token_terms(CHUNK, 2 * CHUNK)
    start(pair[1])
    start(pair[2])

    lo, hi = pl.ds(0, half), pl.ds(half, half)
    mine_row = pl.multiple_of(c * (SIDE * LOCAL), SIDE * LOCAL)

    def rows_of(q):
        return pl.ds(q * CHUNK + mine_row, SIDE * LOCAL)

    def add(dst, rows, lanes, *others):
        def body(n, carry):
            here = pl.ds(pl.multiple_of(rows.start + n * LOCAL, LOCAL), LOCAL)
            there = pl.ds(pl.multiple_of(n * LOCAL, LOCAL), LOCAL)
            total = dst[here, lanes].astype(F32)
            for one, cut in others:
                total += one[there, cut].astype(F32)
            dst[here, lanes] = total.astype(BF16)
            return carry

        lax.fori_loop(0, rows.size // LOCAL, body, 0)

    def pair_sum(q):
        pair[q].wait_recv()
        add(tg, rows_of(q), lo, (pair_in.at[q], lo))
        add(tg, rows_of(q), hi, (pair_in.at[q], hi))

    all_of = pl.ds(0, half)
    far_b = (
        copy(tg.at[rows_of(3), lo], half_b.at[0], at(0, 1)),
        copy(tg.at[rows_of(3), hi], half_b.at[1], at(0, 3)),
    )
    near_b = (
        copy(tg.at[rows_of(1), hi], half_b.at[2], at(0, 1)),
        copy(tg.at[rows_of(2), lo], half_b.at[3], at(0, 3)),
        copy(tg.at[rows_of(1), lo], half_b.at[4], at(0, 1)),
        copy(tg.at[rows_of(2), hi], half_b.at[5], at(0, 3)),
    )
    pair_sum(3)
    start(far_b[0])
    start(far_b[1])
    pair_sum(1)
    start(near_b[0])
    pair_sum(2)
    start(near_b[1])
    far_b[0].wait_recv()
    add(tg, rows_of(1), lo, (half_b.at[0], all_of))
    start(near_b[2])
    far_b[1].wait_recv()
    add(tg, rows_of(2), hi, (half_b.at[1], all_of))
    start(near_b[3])
    pair_sum(0)

    for i in (0, 3, 1, 2):
        bx.got_b(i, 3)
        bd.got_b(i, 1)
        bx.got_b(i, 1)
        bd.got_b(i, 3)
    pass_deltas(2)
    for one in near_b:
        one.wait_recv()
    add(tg, rows_of(0), lo, (half_b.at[3], all_of), (half_b.at[4], all_of))
    add(tg, rows_of(0), hi, (half_b.at[2], all_of), (half_b.at[5], all_of))

    def seat(i):
        return pl.ds(mine_row + i * LOCAL, LOCAL)

    far_a = (
        copy(tg.at[seat(2), lo], half_a.at[0], at(1, 0)),
        copy(tg.at[seat(2), hi], half_a.at[1], at(3, 0)),
    )
    near_a = (
        copy(tg.at[seat(1), hi], half_a.at[2], at(1, 0)),
        copy(tg.at[seat(3), lo], half_a.at[3], at(3, 0)),
        copy(tg.at[seat(1), lo], half_a.at[4], at(1, 0)),
        copy(tg.at[seat(3), hi], half_a.at[5], at(3, 0)),
    )
    start(far_a[0])
    start(far_a[1])
    start(near_a[0])
    start(near_a[1])
    far_a[0].wait_recv()
    add(tg, seat(1), lo, (half_a.at[0], all_of))
    start(near_a[2])
    far_a[1].wait_recv()
    add(tg, seat(3), hi, (half_a.at[1], all_of))
    start(near_a[3])

    for i in (0, 3, 1, 2):
        bx.got_b(i, 2)
        bd.got_b(i, 2)
    pass_deltas(3)
    for one in near_a:
        one.wait_recv()
    mine = tg[seat(0), lo].astype(F32)
    mine += half_a[3].astype(F32)
    mine += half_a[4].astype(F32)
    token_out[:, lo] = mine.astype(BF16)
    mine = tg[seat(0), hi].astype(F32)
    mine += half_a[2].astype(F32)
    mine += half_a[5].astype(F32)
    token_out[:, hi] = mine.astype(BF16)
    for j in range(SIDE):
        bx.got_s(j)
        bd.got_s(j)
    for q in range(SIDE):
        ring[q][2].wait_recv()
        ring[q][3].wait_recv()
        for one in ring[q][4:]:
            one.wait()
    bx_own.wait()
    bd_own.wait()
    for one in started:
        one.wait_send()


COPIES = 31 * 4 + 6 + 16 + 4 + 6 + 6


def fused(tokens, out_grad, prob, w_gate, w_up, w_down):
    local, width = tokens.shape
    hs = w_gate.shape[2]
    part = width // GROUPS
    gtok = local * SLOTS
    anywhere = pl.BlockSpec(memory_space=pl.ANY)
    vmem = pl.BlockSpec(memory_space=pltpu.VMEM)
    flops = 2 * gtok * width * hs * 10
    return pl.pallas_call(
        kernel,
        out_shape=(
            jax.ShapeDtypeStruct((local, width), BF16),
            jax.ShapeDtypeStruct((gtok, EXPERTS), F32),
            jax.ShapeDtypeStruct((2, SIDE, GROUPS, CHUNK, part), BF16),
            jax.ShapeDtypeStruct((SIDE, GROUPS, CHUNK, 6 * hs), BF16),
        ),
        in_specs=[anywhere, anywhere, vmem, anywhere, anywhere, anywhere],
        out_specs=(vmem, vmem, anywhere, anywhere),
        scratch_shapes=[
            pltpu.VMEM((gtok, width), BF16),
            pltpu.VMEM((gtok, width), BF16),
            pltpu.VMEM(w_gate.shape, BF16),
            pltpu.VMEM(w_up.shape, BF16),
            pltpu.VMEM(w_down.shape, BF16),
            pltpu.VMEM((gtok, 6 * hs), BF16),
            pltpu.VMEM((gtok, width), BF16),
            pltpu.VMEM((SIDE, SIDE * LOCAL, width), BF16),
            pltpu.VMEM((6, SIDE * LOCAL, width // 2), BF16),
            pltpu.VMEM((6, LOCAL, width // 2), BF16),
            pltpu.VMEM((2, GROUPS - 1, LOCAL, part), BF16),
            pltpu.SemaphoreType.DMA((19,)),
            pltpu.SemaphoreType.DMA((COPIES,)),
            pltpu.SemaphoreType.DMA((COPIES,)),
        ],
        compiler_params=pltpu.CompilerParams(
            collective_id=0, has_side_effects=True, vmem_limit_bytes=60 << 20
        ),
        cost_estimate=pl.CostEstimate(flops=flops, bytes_accessed=60 << 20, transcendentals=0),
    )(tokens, out_grad, prob, w_gate, w_up, w_down)


def shards(tokens, out_grad, row_prob, row_token, block_expert, w_gate, w_up, w_down):
    local, width = tokens.shape[1:]
    gtok = local * SLOTS
    hs = w_gate.shape[2]

    y, z, c = place()
    source = jnp.arange(SLOTS, dtype=jnp.int32)
    sy, sz, sc = source // (2 * SIDE), (source // 2) % SIDE, source % 2
    dy_, dz_ = (sy - y) % SIDE, (sz - z) % SIDE
    i = jnp.where(sc == 0, dy_, dz_)
    j = jnp.where(sc == 0, dz_, dy_)
    chunk = jnp.where(j == 2, 3, jnp.where(j == 3, 2, j))
    slot_of = chunk * 8 + sc * SIDE + i
    row_of = (slot_of[:, None] * LOCAL + jnp.arange(LOCAL, dtype=jnp.int32)[None, :]).reshape(-1)
    row_expert = jnp.repeat(block_expert[0], BLOCK)
    token = row_token[0]
    safe = jnp.minimum(token, gtok - 1)
    row = jnp.where(token < gtok, row_of[safe], gtok)
    hit = row[:, None] == jnp.arange(gtok, dtype=jnp.int32)[None, :]
    prob = jnp.stack(
        [
            jnp.sum(jnp.where(hit & (row_expert == e)[:, None], row_prob[0][:, None], 0.0), axis=0)
            for e in range(EXPERTS)
        ],
        axis=1,
    )
    token_sum, prob_part, cols, deltas = fused(
        tokens[0], out_grad[0], prob, w_gate, w_up, w_down
    )
    mine = jnp.where((row_expert == 0)[:, None], prob_part[:, 0][None], prob_part[:, 1][None])
    prob_rows = jnp.sum(jnp.where(hit, mine, 0.0), axis=1)
    prob_sum = jnp.sum(lax.all_gather(prob_rows, "fsdp", axis=0), axis=0)

    xc = cols[0].reshape(gtok * GROUPS, width // GROUPS)
    dyc = cols[1].reshape(gtok * GROUPS, width // GROUPS)
    every = deltas.reshape(gtok * GROUPS, 6 * hs)

    def piece(k):
        return every[:, k * hs : (k + 1) * hs]

    gate_grad = jnp.stack([dot(xc, piece(2 * e), 0, 0).astype(BF16) for e in range(EXPERTS)])
    up_grad = jnp.stack([dot(xc, piece(2 * e + 1), 0, 0).astype(BF16) for e in range(EXPERTS)])
    down_grad = jnp.stack([dot(piece(4 + e), dyc, 0, 0).astype(BF16) for e in range(EXPERTS)])
    return (token_sum[None], prob_sum[None], gate_grad, up_grad, down_grad)


def solution(mesh):
    in_specs = (
        P("dp", "fsdp", None),
        P("dp", "fsdp", None),
        P("dp", None),
        P("dp", None),
        P("dp", None),
        P(None, None, "fsdp"),
        P(None, None, "fsdp"),
        P(None, "fsdp", None),
    )
    out_specs = (
        P("dp", "fsdp", None),
        P("dp", None),
        P(None, "dp", "fsdp"),
        P(None, "dp", "fsdp"),
        P(None, "fsdp", "dp"),
    )
    return jax.shard_map(shards, mesh=mesh, in_specs=in_specs, out_specs=out_specs, check_vma=False)
```

```python
import functools

import jax
import jax.numpy as jnp
from jax import lax
from jax.experimental import pallas as pl
from jax.experimental.pallas import tpu as pltpu
from jax.sharding import PartitionSpec as P

EXPERTS = 2
BLOCK = 128
SIDE = 4
GROUPS = 4
LOCAL = 16
SLOTS = 32
CHUNK = 128
CORE_ROWS = CHUNK // 2
PIECE = CORE_ROWS // 2
ORDER = (0, 3, 1, 2)
SEAT = (0, 2, 3, 1)
BF16 = jnp.bfloat16
F32 = jnp.float32


def dot(a, b, ca, cb):
    return lax.dot_general(a, b, (((ca,), (cb,)), ((), ())), preferred_element_type=F32)


def offset_row(i, j):
    seat = SEAT[i]
    if j == 0:
        return seat * LOCAL
    if j == 2:
        return 3 * CHUNK + seat * LOCAL
    return (1 + seat // 2) * CHUNK + (j // 2) * PIECE + (seat % 2) * LOCAL


def place():
    f = lax.axis_index("fsdp")
    return f // (2 * SIDE), (f // 2) % SIDE, f % 2


def kernel(
    tokens, out_grad, prob, w_gate, w_up, w_down,
    token_out, prob_out, gate_out, up_out, down_out, cols,
    xs, dys, wgu, wd, deltas, pair_in, half_b, half_a, stage, held, acc, acc_down,
    share_c, share_y, share_z, local_sem, send, recv,
):
    y, z, c = place()
    p = lax.axis_index("dp")
    width = xs.shape[1]
    half = width // 2
    part = width // GROUPS
    hs = wd.shape[1]
    count = [0]
    locals_ = [0]

    def device(yy, zz, cc):
        return {"fsdp": ((yy % SIDE) * SIDE + zz % SIDE) * 2 + cc}

    def at(da, db):
        return device(y + (1 - c) * da + c * db, z + c * da + (1 - c) * db, c)

    sibling = device(y, z, 1 - c)

    def over(k):
        return {"dp": (p + k) % GROUPS}

    barrier = pltpu.get_barrier_semaphore()
    peers = [at(1, 0), at(2, 0), at(3, 0), at(0, 1), at(0, 2), at(0, 3), sibling]
    peers += [over(1), over(2), over(3)]
    for peer in peers:
        pl.semaphore_signal(barrier, inc=1, device_id=peer, device_id_type=pl.DeviceIdType.MESH)
    pl.semaphore_wait(barrier, len(peers))

    unsent = []

    def copy(src, dst, to):
        n = count[0]
        count[0] += 1
        return pltpu.make_async_remote_copy(
            src_ref=src, dst_ref=dst, send_sem=send.at[n], recv_sem=recv.at[n],
            device_id=to, device_id_type=pl.DeviceIdType.MESH,
        )

    def local(src, dst):
        n = locals_[0]
        locals_[0] += 1
        return pltpu.make_async_copy(src, dst, local_sem.at[n])

    def start(one):
        one.start()
        unsent.append(one)

    def sent(ones):
        for one in ones:
            one.wait_send()
            unsent[:] = [copied for copied in unsent if copied is not one]

    core_row = pl.multiple_of(c * CORE_ROWS, CORE_ROWS)
    other_row = pl.multiple_of((1 - c) * CORE_ROWS, CORE_ROWS)

    def slot_row(i, j):
        return pl.multiple_of(core_row + offset_row(i, j), LOCAL)

    class Gather:
        def __init__(self, slot, mine, plus):
            far = 3 if plus else 1
            self.plus, self.far = plus, far
            self.a = {3: copy(mine, slot(3, 0), at(1, 0)), 1: copy(mine, slot(1, 0), at(3, 0))}
            self.a[2] = copy(slot(far, 0), slot(2, 0), at(1 if plus else 3, 0))
            self.b, self.s = {}, {}
            for i in range(SIDE):
                src = mine if i == 0 else slot(i, 0)
                self.b[i, 3] = copy(src, slot(i, 3), at(0, 1))
                self.b[i, 1] = copy(src, slot(i, 1), at(0, 3))
                self.b[i, 2] = copy(slot(i, far), slot(i, 2), at(0, 1 if plus else 3))
                for j in range(SIDE):
                    src = mine if i == 0 and j == 0 else slot(i, j)
                    self.s[i, j] = copy(src, slot(i, j), sibling)

        def begin_a(self):
            start(self.a[3])
            start(self.a[1])

        def begin_b(self):
            start(self.b[0, 3])
            start(self.b[0, 1])
            start(self.s[0, 0])

        def got_a(self, i):
            self.a[i].wait_recv()
            if i == self.far:
                start(self.a[2])
            start(self.b[i, 3])
            start(self.b[i, 1])
            start(self.s[i, 0])

        def got_b(self, i, j):
            self.b[i, j].wait_recv()
            if j == self.far:
                start(self.b[i, 2])
            start(self.s[i, j])

        def got_s(self, *slots):
            for slot in slots:
                self.s[slot].wait_recv()

        def from_chunk(self, q):
            if q == 0:
                ones = [self.a[2]] + [self.b[i, j] for i in (1, 2, 3) for j in (1, 3)]
                return ones + [self.s[i, 0] for i in (1, 2, 3)]
            if q == 3:
                return [self.s[i, 2] for i in range(SIDE)]
            ones = []
            for i in ORDER[2 * q - 2 : 2 * q]:
                ones += [self.b[i, 2], self.s[i, 1], self.s[i, 3]]
            return ones

    zero = [(i, 0) for i in range(SIDE)]
    near = [[(i, j) for i in ORDER[2 * u : 2 * u + 2] for j in (1, 3)] for u in range(2)]
    far = [(i, 2) for i in range(SIDE)]
    chunk_slots = [zero, near[0], near[1], far]

    def chunk_rows(q):
        return pl.ds(q * CHUNK, CHUNK)

    row0 = slot_row(0, 0)
    fill = [
        local(tokens, xs.at[pl.ds(row0, LOCAL)]),
        local(out_grad, dys.at[pl.ds(row0, LOCAL)]),
        local(w_gate.at[0], wgu.at[:, pl.ds(0, hs)]),
        local(w_up.at[0], wgu.at[:, pl.ds(hs, hs)]),
        local(w_down, wd),
        local(w_gate.at[1], wgu.at[:, pl.ds(2 * hs, hs)]),
        local(w_up.at[1], wgu.at[:, pl.ds(3 * hs, hs)]),
    ]
    ax = Gather(lambda i, j: xs.at[pl.ds(slot_row(i, j), LOCAL)], tokens, True)
    ad = Gather(lambda i, j: dys.at[pl.ds(slot_row(i, j), LOCAL)], out_grad, False)

    def col_slot(k):
        def slot(i, j):
            row = offset_row(i, j)
            rows = pl.ds(pl.multiple_of(core_row + row % CHUNK, LOCAL), LOCAL)
            return cols.at[k, row // CHUNK, pl.ds(1, GROUPS - 1), rows]

        return slot

    bx = Gather(col_slot(0), stage.at[0], True)
    bd = Gather(col_slot(1), stage.at[1], False)
    swaps = []
    for k, src in enumerate((tokens, out_grad)):
        for step in range(1, GROUPS):
            lane = pl.multiple_of(((p + step) % GROUPS) * part, part)
            swaps.append(
                copy(src.at[:, pl.ds(lane, part)], stage.at[k, GROUPS - step - 1], over(step))
            )

    ring, own_cols, load = {}, {}, {}
    lane = pl.multiple_of(p * part, part)
    for q in range(SIDE):
        top, bottom = pl.ds(0, CHUNK // 2), pl.ds(CHUNK // 2, CHUNK // 2)
        ring[q] = (
            copy(deltas.at[q, 0], deltas.at[q, 3], over(1)),
            copy(deltas.at[q, 0], deltas.at[q, 1], over(3)),
            copy(deltas.at[q, 3, top], deltas.at[q, 2, top], over(1)),
            copy(deltas.at[q, 1, bottom], deltas.at[q, 2, bottom], over(3)),
        )
        own_cols[q] = (
            local(xs.at[chunk_rows(q), pl.ds(lane, part)], cols.at[0, q, 0]),
            local(dys.at[chunk_rows(q), pl.ds(lane, part)], cols.at[1, q, 0]),
        )
        load[q] = local(cols.at[:, q], held)
    stage_own = [local(stage.at[k], col_slot(k)(0, 0)) for k in range(2)]

    def forward(q):
        where = chunk_rows(q)
        for e in range(EXPERTS):
            gate_up = dot(xs[where], wgu[:, 2 * e * hs : (2 * e + 2) * hs], 1, 0)
            gate, up = gate_up[:, :hs], gate_up[:, hs:]
            back = dot(dys[where], wd[e], 1, 1)
            sigma = jax.nn.sigmoid(gate)
            silu = gate * sigma
            hidden = (silu * up).astype(BF16).astype(F32)
            product = hidden * back
            folded = product[:, : hs // 2] + product[:, hs // 2 :]
            row = jnp.sum(jnp.transpose(folded), axis=0, keepdims=True)
            for k in range(2):
                for i, j in chunk_slots[q]:
                    first = k * CORE_ROWS + offset_row(i, j) % CHUNK
                    owner = device(y + (1 - k) * i + k * j, z + k * i + (1 - k) * j, k)["fsdp"]
                    share_c[c, pl.ds(owner, 1), e * LOCAL : (e + 1) * LOCAL] = row[
                        :, first : first + LOCAL
                    ]
            share = prob[where, e : e + 1]
            scaled = share * back
            slope = sigma * (1.0 + gate * (1.0 - sigma))
            deltas[q, 0, :, 2 * e * hs : (2 * e + 1) * hs] = (scaled * up * slope).astype(BF16)
            deltas[q, 0, :, (2 * e + 1) * hs : (2 * e + 2) * hs] = (scaled * silu).astype(BF16)
            deltas[q, 0, :, (4 + e) * hs : (5 + e) * hs] = (share * hidden).astype(BF16)

    def token_terms(q):
        step = 512
        where = chunk_rows(q)

        def body(n, carry):
            at_n = pl.ds(pl.multiple_of(n * step, step), step)
            total = dot(deltas[q, 0, :, 0 : 4 * hs], wgu[at_n, :], 1, 1)
            dys[where, at_n] = total.astype(BF16)
            return carry

        lax.fori_loop(0, width // step, body, 0)

    def start_own_cols(q):
        for one in own_cols[q]:
            one.start()

    def send_deltas(q):
        start(ring[q][0])
        start(ring[q][1])

    def pass_deltas(q):
        ring[q][0].wait_recv()
        start(ring[q][2])
        ring[q][1].wait_recv()
        start(ring[q][3])

    tile = 256
    drain = []

    def load_cols(q):
        bx.got_s(*chunk_slots[q])
        bd.got_s(*chunk_slots[q])
        if q == 0:
            for one in stage_own:
                one.wait()
        load[q].start()

    def weight_terms(q, first=False, last=False):
        ring[q][2].wait_recv()
        ring[q][3].wait_recv()
        load[q].wait()
        rows = GROUPS * CHUNK
        delta = deltas.at[q]

        def one_tile(n):
            lanes = pl.ds(pl.multiple_of(n * tile, tile), tile)
            x = held[0, :, :, lanes].reshape(rows, tile)
            return lanes, dot(x, delta[:, :, 0 : 4 * hs].reshape(rows, 4 * hs), 0, 0)

        def body(n, carry):
            lanes, term = one_tile(n)
            if first:
                acc[lanes, :] = term
            else:
                acc[lanes, :] += term
            return carry

        if not last:
            lax.fori_loop(0, part // tile, body, 0)
        else:
            for n in range(part // tile):
                lanes, term = one_tile(n)
                total = (acc[n * tile : (n + 1) * tile, :] + term).astype(BF16)
                up_row, left = (n % 2) * tile, (n // 2) * 4 * hs
                xs[up_row : up_row + tile, left : left + 4 * hs] = total
                for e in range(EXPERTS):
                    for k, out in enumerate((gate_out, up_out)):
                        src = xs.at[
                            pl.ds(up_row, tile), pl.ds(left + (2 * e + k) * hs, hs)
                        ]
                        drain.append(local(src, out.at[e, pl.ds(n * tile, tile)]))
                        drain[-1].start()
        for e in range(EXPERTS):
            term = dot(
                delta[:, :, (4 + e) * hs : (5 + e) * hs].reshape(rows, hs),
                held[1].reshape(rows, part), 0, 0,
            )
            if first:
                acc_down[e] = term
            elif not last:
                acc_down[e] += term
            else:
                left = 3 * 4 * hs
                xs[e * hs : (e + 1) * hs, left : left + part] = (acc_down[e] + term).astype(BF16)
                src = xs.at[pl.ds(e * hs, hs), pl.ds(left, part)]
                drain.append(local(src, down_out.at[e]))
                drain[-1].start()

    pair = [
        copy(dys.at[pl.ds(q * CHUNK + other_row, CORE_ROWS)], pair_in.at[q], sibling)
        for q in range(SIDE)
    ]
    lo, hi = pl.ds(0, half), pl.ds(half, half)

    def piece(q, u):
        return pl.ds(q * CHUNK + core_row + u * PIECE, PIECE)

    def add(rows, lanes, *others):
        def body(n, carry):
            here = pl.ds(pl.multiple_of(rows.start + n * LOCAL, LOCAL), LOCAL)
            there = pl.ds(pl.multiple_of(n * LOCAL, LOCAL), LOCAL)
            total = dys[here, lanes].astype(F32)
            for one, cut in others:
                total += one[there, cut].astype(F32)
            dys[here, lanes] = total.astype(BF16)
            return carry

        lax.fori_loop(0, rows.size // LOCAL, body, 0)

    def pair_sum(q):
        pair[q].wait_recv()
        rows = pl.ds(q * CHUNK + core_row, CORE_ROWS)
        add(rows, lo, (pair_in.at[q], lo))
        add(rows, hi, (pair_in.at[q], hi))

    whole = pl.ds(0, half)
    far_b = [
        (
            copy(dys.at[piece(3, u), lo], half_b.at[u, 0], at(0, 1)),
            copy(dys.at[piece(3, u), hi], half_b.at[u, 1], at(0, 3)),
        )
        for u in range(2)
    ]
    near_b = [
        (
            copy(dys.at[piece(1 + u, 0), hi], half_b.at[u, 2], at(0, 1)),
            copy(dys.at[piece(1 + u, 1), lo], half_b.at[u, 3], at(0, 3)),
            copy(dys.at[piece(1 + u, 0), lo], half_b.at[u, 4], at(0, 1)),
            copy(dys.at[piece(1 + u, 1), hi], half_b.at[u, 5], at(0, 3)),
        )
        for u in range(2)
    ]

    def far_to_near(u):
        far_b[u][0].wait_recv()
        add(piece(1 + u, 0), lo, (half_b.at[u, 0], whole))
        start(near_b[u][2])
        far_b[u][1].wait_recv()
        add(piece(1 + u, 1), hi, (half_b.at[u, 1], whole))
        start(near_b[u][3])

    def near_to_mine(u):
        for one in near_b[u]:
            one.wait_recv()
        add(piece(0, u), lo, (half_b.at[u, 3], whole), (half_b.at[u, 4], whole))
        add(piece(0, u), hi, (half_b.at[u, 2], whole), (half_b.at[u, 5], whole))

    def seat(i):
        return pl.ds(slot_row(i, 0), LOCAL)

    far_a = (
        copy(dys.at[seat(2), lo], half_a.at[0], at(1, 0)),
        copy(dys.at[seat(2), hi], half_a.at[1], at(3, 0)),
    )
    near_a = (
        copy(dys.at[seat(1), hi], half_a.at[2], at(1, 0)),
        copy(dys.at[seat(3), lo], half_a.at[3], at(3, 0)),
        copy(dys.at[seat(1), lo], half_a.at[4], at(1, 0)),
        copy(dys.at[seat(3), hi], half_a.at[5], at(3, 0)),
    )

    to_c = copy(share_c.at[c], share_c.at[c], sibling)
    to_y = [copy(share_y.at[y], share_y.at[y], device(y + k, z, c)) for k in range(1, SIDE)]
    to_z = [copy(share_z.at[z], share_z.at[z], device(y, z + k, c)) for k in range(1, SIDE)]

    def prob_y():
        to_c.wait_recv()
        share_y[y] = share_c[0] + share_c[1]
        for one in to_y:
            start(one)

    def prob_z():
        for one in to_y:
            one.wait_recv()
        share_z[z] = (share_y[0] + share_y[1]) + (share_y[2] + share_y[3])
        for one in to_z:
            start(one)

    def prob_end():
        for one in to_z:
            one.wait_recv()
        prob_out[...] = (share_z[0] + share_z[1]) + (share_z[2] + share_z[3])

    def near_shards(x, d, u):
        for i in ORDER[2 * u : 2 * u + 2]:
            x.got_b(i, 3)
            d.got_b(i, 1)
            x.got_b(i, 1)
            d.got_b(i, 3)

    def far_shards(x, d):
        for i in ORDER:
            x.got_b(i, 2)
            d.got_b(i, 2)

    def first_shards(x, d):
        x.got_a(3)
        d.got_a(1)
        x.got_a(1)
        d.got_a(3)

    ax.begin_a()
    ad.begin_a()
    for one in fill:
        one.start()
    for one in swaps:
        start(one)
    ax.begin_b()
    ad.begin_b()
    share_c[c] = jnp.zeros(share_c.shape[1:], F32)
    first_shards(ax, ad)
    ax.got_a(2)
    ad.got_a(2)
    for one in fill:
        one.wait()
    ax.got_s(*zero)
    ad.got_s(*zero)
    start_own_cols(0)
    forward(0)
    send_deltas(0)
    for one in swaps:
        one.wait_recv()
    for one in stage_own:
        one.start()
    bx.begin_a()
    bd.begin_a()

    near_shards(ax, ad, 0)
    ax.got_s(*near[0])
    ad.got_s(*near[0])
    start_own_cols(1)
    forward(1)
    send_deltas(1)
    near_shards(ax, ad, 1)
    bx.begin_b()
    bd.begin_b()
    first_shards(bx, bd)
    ax.got_s(*near[1])
    ad.got_s(*near[1])
    start_own_cols(2)
    forward(2)
    send_deltas(2)
    pass_deltas(0)

    far_shards(ax, ad)
    bx.got_a(2)
    bd.got_a(2)
    ax.got_s(*far)
    ad.got_s(*far)
    start_own_cols(3)
    forward(3)
    send_deltas(3)
    start(to_c)

    def token_part(q):
        sent(ad.from_chunk(q))
        for one in own_cols[q]:
            one.wait()
        token_terms(q)
        start(pair[q])

    token_part(3)
    near_shards(bx, bd, 0)
    token_part(1)
    pair_sum(3)
    for u in range(2):
        start(far_b[u][0])
        start(far_b[u][1])
    prob_y()
    pair_sum(1)
    start(near_b[0][0])
    start(near_b[0][1])
    pass_deltas(1)
    token_part(2)
    near_shards(bx, bd, 1)
    pair_sum(2)
    start(near_b[1][0])
    start(near_b[1][1])
    prob_z()
    far_to_near(0)
    far_to_near(1)
    token_part(0)
    load_cols(0)
    pass_deltas(2)
    prob_end()
    pair_sum(0)
    weight_terms(0, first=True)
    far_shards(bx, bd)
    load_cols(1)
    near_to_mine(0)
    near_to_mine(1)
    start(far_a[0])
    start(far_a[1])
    start(near_a[0])
    start(near_a[1])
    weight_terms(1)
    load_cols(2)
    far_a[0].wait_recv()
    add(seat(1), lo, (half_a.at[0], whole))
    start(near_a[2])
    far_a[1].wait_recv()
    add(seat(3), hi, (half_a.at[1], whole))
    start(near_a[3])
    pass_deltas(3)
    weight_terms(2)
    load_cols(3)
    for one in near_a:
        one.wait_recv()
    mine = dys[seat(0), lo].astype(F32)
    mine += half_a[3].astype(F32)
    mine += half_a[4].astype(F32)
    token_out[:, lo] = mine.astype(BF16)
    mine = dys[seat(0), hi].astype(F32)
    mine += half_a[2].astype(F32)
    mine += half_a[5].astype(F32)
    token_out[:, hi] = mine.astype(BF16)
    sent(list(unsent))
    weight_terms(3, last=True)
    for one in drain:
        one.wait()


COPIES = 31 * 4 + 6 + 16 + 4 + 12 + 6 + 7
LOCALS = 7 + 12 + 2 + 26


def fused(tokens, out_grad, prob, w_gate, w_up, w_down):
    local, width = tokens.shape
    hs = w_gate.shape[2]
    part = width // GROUPS
    gtok = local * SLOTS
    anywhere = pl.BlockSpec(memory_space=pl.ANY)
    vmem = pl.BlockSpec(memory_space=pltpu.VMEM)
    flops = 2 * gtok * width * hs * 16
    return pl.pallas_call(
        kernel,
        out_shape=(
            jax.ShapeDtypeStruct((local, width), BF16),
            jax.ShapeDtypeStruct((SLOTS, 128), F32),
            jax.ShapeDtypeStruct((EXPERTS, part, hs), BF16),
            jax.ShapeDtypeStruct((EXPERTS, part, hs), BF16),
            jax.ShapeDtypeStruct((EXPERTS, hs, part), BF16),
            jax.ShapeDtypeStruct((2, SIDE, GROUPS, CHUNK, part), BF16),
        ),
        in_specs=[anywhere, anywhere, vmem, anywhere, anywhere, anywhere],
        out_specs=(vmem, vmem, anywhere, anywhere, anywhere, anywhere),
        scratch_shapes=[
            pltpu.VMEM((gtok, width), BF16),
            pltpu.VMEM((gtok, width), BF16),
            pltpu.VMEM((width, 4 * hs), BF16),
            pltpu.VMEM(w_down.shape, BF16),
            pltpu.VMEM((SIDE, GROUPS, CHUNK, 6 * hs), BF16),
            pltpu.VMEM((SIDE, CORE_ROWS, width), BF16),
            pltpu.VMEM((2, 6, PIECE, width // 2), BF16),
            pltpu.VMEM((6, LOCAL, width // 2), BF16),
            pltpu.VMEM((2, GROUPS - 1, LOCAL, part), BF16),
            pltpu.VMEM((2, GROUPS, CHUNK, part), BF16),
            pltpu.VMEM((part, 4 * hs), F32),
            pltpu.VMEM((EXPERTS, hs, part), F32),
            pltpu.VMEM((2, SLOTS, 128), F32),
            pltpu.VMEM((SIDE, SLOTS, 128), F32),
            pltpu.VMEM((SIDE, SLOTS, 128), F32),
            pltpu.SemaphoreType.DMA((LOCALS,)),
            pltpu.SemaphoreType.DMA((COPIES,)),
            pltpu.SemaphoreType.DMA((COPIES,)),
        ],
        compiler_params=pltpu.CompilerParams(
            collective_id=0, has_side_effects=True, vmem_limit_bytes=62 << 20
        ),
        cost_estimate=pl.CostEstimate(flops=flops, bytes_accessed=60 << 20, transcendentals=0),
    )(tokens, out_grad, prob, w_gate, w_up, w_down)


def shards(tokens, out_grad, row_prob, row_token, block_expert, w_gate, w_up, w_down):
    local, width = tokens.shape[1:]
    gtok = local * SLOTS
    row_expert = jnp.repeat(block_expert[0], BLOCK)
    token = row_token[0]

    y, z, c = place()
    source = token // LOCAL
    off_y = (source // (2 * SIDE) - y) % SIDE
    off_z = ((source // 2) % SIDE - z) % SIDE
    core = source % 2
    i = jnp.where(core == 0, off_y, off_z)
    j = jnp.where(core == 0, off_z, off_y)
    seat = jnp.where(i == 0, 0, jnp.where(i == 3, 1, i + 1))
    near = (1 + seat // 2) * CHUNK + (j // 2) * PIECE + (seat % 2) * LOCAL
    row = jnp.where(j % 2 == 1, near, (j // 2) * 3 * CHUNK + seat * LOCAL)
    row = jnp.where(token < gtok, row + core * CORE_ROWS + token % LOCAL, gtok)
    every = jnp.arange(gtok, dtype=jnp.int32)[None, :]
    hit = row[:, None] == every
    prob = jnp.stack(
        [
            jnp.sum(jnp.where(hit & (row_expert == e)[:, None], row_prob[0][:, None], 0.0), axis=0)
            for e in range(EXPERTS)
        ],
        axis=1,
    )
    token_sum, prob_total, gate_grad, up_grad, down_grad, _ = fused(
        tokens[0], out_grad[0], prob, w_gate, w_up, w_down
    )
    prob_tok = [prob_total[:, e * LOCAL : (e + 1) * LOCAL].reshape(gtok) for e in range(EXPERTS)]
    mine = jnp.where((row_expert == 0)[:, None], prob_tok[0][None], prob_tok[1][None])
    prob_sum = jnp.sum(jnp.where(token[:, None] == every, mine, 0.0), axis=1)
    return (token_sum[None], prob_sum[None], gate_grad, up_grad, down_grad)


def solution(mesh):
    in_specs = (
        P("dp", "fsdp", None),
        P("dp", "fsdp", None),
        P("dp", None),
        P("dp", None),
        P("dp", None),
        P(None, None, "fsdp"),
        P(None, None, "fsdp"),
        P(None, "fsdp", None),
    )
    out_specs = (
        P("dp", "fsdp", None),
        P("dp", None),
        P(None, "dp", "fsdp"),
        P(None, "dp", "fsdp"),
        P(None, "fsdp", "dp"),
    )
    return jax.shard_map(shards, mesh=mesh, in_specs=in_specs, out_specs=out_specs, check_vma=False)
```

```python
import functools

import jax
import jax.numpy as jnp
from jax import lax
from jax.experimental import pallas as pl
from jax.experimental.pallas import tpu as pltpu
from jax.sharding import PartitionSpec as P

EXPERTS = 2
BLOCK = 128
SIDE = 4
GROUPS = 4
LOCAL = 16
SLOTS = 32
CHUNK = 128
CORE_ROWS = CHUNK // 2
PIECE = CORE_ROWS // 2
ORDER = (0, 3, 1, 2)
SEAT = (0, 2, 3, 1)
BF16 = jnp.bfloat16
F32 = jnp.float32


def dot(a, b, ca, cb):
    return lax.dot_general(a, b, (((ca,), (cb,)), ((), ())), preferred_element_type=F32)


def offset_row(i, j):
    seat = SEAT[i]
    if j == 0:
        return seat * LOCAL
    if j == 2:
        return 3 * CHUNK + seat * LOCAL
    return (1 + seat // 2) * CHUNK + (j // 2) * PIECE + (seat % 2) * LOCAL


def place():
    f = lax.axis_index("fsdp")
    return f // (2 * SIDE), (f // 2) % SIDE, f % 2


def kernel(
    tokens, out_grad, prob, w_gate, w_up, w_down,
    token_out, prob_out, gate_out, up_out, down_out, cols,
    xs, dys, wgu, wd, deltas, pair_in, half_b, half_a, stage, held, first_tg, acc, acc_down,
    share_c, share_y, share_z, local_sem, send, recv,
):
    y, z, c = place()
    p = lax.axis_index("dp")
    width = xs.shape[1]
    half = width // 2
    part = width // GROUPS
    hs = wd.shape[1]
    count = [0]
    locals_ = [0]

    def device(yy, zz, cc):
        return {"fsdp": ((yy % SIDE) * SIDE + zz % SIDE) * 2 + cc}

    def at(da, db):
        return device(y + (1 - c) * da + c * db, z + c * da + (1 - c) * db, c)

    sibling = device(y, z, 1 - c)

    def over(k):
        return {"dp": (p + k) % GROUPS}

    barrier = pltpu.get_barrier_semaphore()
    peers = [at(1, 0), at(2, 0), at(3, 0), at(0, 1), at(0, 2), at(0, 3), sibling]
    peers += [over(1), over(2), over(3)]
    for peer in peers:
        pl.semaphore_signal(barrier, inc=1, device_id=peer, device_id_type=pl.DeviceIdType.MESH)
    pl.semaphore_wait(barrier, len(peers))

    unsent = []

    def copy(src, dst, to):
        n = count[0]
        count[0] += 1
        return pltpu.make_async_remote_copy(
            src_ref=src, dst_ref=dst, send_sem=send.at[n], recv_sem=recv.at[n],
            device_id=to, device_id_type=pl.DeviceIdType.MESH,
        )

    def local(src, dst):
        n = locals_[0]
        locals_[0] += 1
        return pltpu.make_async_copy(src, dst, local_sem.at[n])

    def start(one):
        one.start()
        unsent.append(one)

    def sent(ones):
        for one in ones:
            one.wait_send()
            unsent[:] = [copied for copied in unsent if copied is not one]

    core_row = pl.multiple_of(c * CORE_ROWS, CORE_ROWS)
    other_row = pl.multiple_of((1 - c) * CORE_ROWS, CORE_ROWS)

    def slot_row(i, j):
        return pl.multiple_of(core_row + offset_row(i, j), LOCAL)

    class Gather:
        def __init__(self, slot, mine, plus):
            far = 3 if plus else 1
            self.plus, self.far = plus, far
            self.a = {3: copy(mine, slot(3, 0), at(1, 0)), 1: copy(mine, slot(1, 0), at(3, 0))}
            self.a[2] = copy(slot(far, 0), slot(2, 0), at(1 if plus else 3, 0))
            self.b, self.s = {}, {}
            for i in range(SIDE):
                src = mine if i == 0 else slot(i, 0)
                self.b[i, 3] = copy(src, slot(i, 3), at(0, 1))
                self.b[i, 1] = copy(src, slot(i, 1), at(0, 3))
                self.b[i, 2] = copy(slot(i, far), slot(i, 2), at(0, 1 if plus else 3))
                for j in range(SIDE):
                    src = mine if i == 0 and j == 0 else slot(i, j)
                    self.s[i, j] = copy(src, slot(i, j), sibling)

        def begin_a(self):
            start(self.a[3])
            start(self.a[1])

        def begin_b(self):
            start(self.b[0, 3])
            start(self.b[0, 1])
            start(self.s[0, 0])

        def got_a(self, i):
            self.a[i].wait_recv()
            if i == self.far:
                start(self.a[2])
            start(self.b[i, 3])
            start(self.b[i, 1])
            start(self.s[i, 0])

        def got_b(self, i, j):
            self.b[i, j].wait_recv()
            if j == self.far:
                start(self.b[i, 2])
            start(self.s[i, j])

        def got_s(self, *slots):
            for slot in slots:
                self.s[slot].wait_recv()

        def from_chunk(self, q):
            if q == 0:
                ones = [self.a[2]] + [self.b[i, j] for i in (1, 2, 3) for j in (1, 3)]
                return ones + [self.s[i, 0] for i in (1, 2, 3)]
            if q == 3:
                return [self.s[i, 2] for i in range(SIDE)]
            ones = []
            for i in ORDER[2 * q - 2 : 2 * q]:
                ones += [self.b[i, 2], self.s[i, 1], self.s[i, 3]]
            return ones

    zero = [(i, 0) for i in range(SIDE)]
    near = [[(i, j) for i in ORDER[2 * u : 2 * u + 2] for j in (1, 3)] for u in range(2)]
    far = [(i, 2) for i in range(SIDE)]
    chunk_slots = [zero, near[0], near[1], far]

    def chunk_rows(q):
        return pl.ds(q * CHUNK, CHUNK)

    row0 = slot_row(0, 0)
    fill = [
        local(tokens, xs.at[pl.ds(row0, LOCAL)]),
        local(out_grad, dys.at[pl.ds(row0, LOCAL)]),
        local(w_gate.at[0], wgu.at[:, pl.ds(0, hs)]),
        local(w_up.at[0], wgu.at[:, pl.ds(hs, hs)]),
        local(w_down, wd),
        local(w_gate.at[1], wgu.at[:, pl.ds(2 * hs, hs)]),
        local(w_up.at[1], wgu.at[:, pl.ds(3 * hs, hs)]),
    ]
    ax = Gather(lambda i, j: xs.at[pl.ds(slot_row(i, j), LOCAL)], tokens, True)
    ad = Gather(lambda i, j: dys.at[pl.ds(slot_row(i, j), LOCAL)], out_grad, False)

    def col_slot(k):
        def slot(i, j):
            row = offset_row(i, j)
            rows = pl.ds(pl.multiple_of(core_row + row % CHUNK, LOCAL), LOCAL)
            return cols.at[k, row // CHUNK, pl.ds(1, GROUPS - 1), rows]

        return slot

    bx = Gather(col_slot(0), stage.at[0], True)
    bd = Gather(col_slot(1), stage.at[1], False)
    swaps = []
    for k, src in enumerate((tokens, out_grad)):
        for step in range(1, GROUPS):
            lane = pl.multiple_of(((p + step) % GROUPS) * part, part)
            swaps.append(
                copy(src.at[:, pl.ds(lane, part)], stage.at[k, GROUPS - step - 1], over(step))
            )

    ring, own_cols, load = {}, {}, {}
    lane = pl.multiple_of(p * part, part)
    for q in range(SIDE):
        ring[q] = []
        for e in range(EXPERTS):
            cut = pl.ds(3 * e * hs, 3 * hs)
            here = deltas.at[q, 0, :, cut]
            passed = deltas.at[q, (3, 1)[e], :, cut]
            ring[q].append(
                (
                    copy(here, deltas.at[q, 3, :, cut], over(1)),
                    copy(here, deltas.at[q, 1, :, cut], over(3)),
                    copy(passed, deltas.at[q, 2, :, cut], over((1, 3)[e])),
                )
            )
        own_cols[q] = (
            local(xs.at[chunk_rows(q), pl.ds(lane, part)], cols.at[0, q, 0]),
            local(dys.at[chunk_rows(q), pl.ds(lane, part)], cols.at[1, q, 0]),
        )
        load[q] = local(cols.at[:, q], held.at[q % 2])
    stage_own = [local(stage.at[k], col_slot(k)(0, 0)) for k in range(2)]

    def forward(q):
        where = chunk_rows(q)
        for e in range(EXPERTS):
            gate_up = dot(xs[where], wgu[:, 2 * e * hs : (2 * e + 2) * hs], 1, 0)
            gate, up = gate_up[:, :hs], gate_up[:, hs:]
            back = dot(dys[where], wd[e], 1, 1)
            sigma = jax.nn.sigmoid(gate)
            silu = gate * sigma
            hidden = (silu * up).astype(BF16).astype(F32)
            product = hidden * back
            folded = product[:, : hs // 2] + product[:, hs // 2 :]
            row = jnp.sum(jnp.transpose(folded), axis=0, keepdims=True)
            for k in range(2):
                for i, j in chunk_slots[q]:
                    first = k * CORE_ROWS + offset_row(i, j) % CHUNK
                    owner = device(y + (1 - k) * i + k * j, z + k * i + (1 - k) * j, k)["fsdp"]
                    share_c[c, pl.ds(owner, 1), e * LOCAL : (e + 1) * LOCAL] = row[
                        :, first : first + LOCAL
                    ]
            share = prob[where, e : e + 1]
            scaled = share * back
            slope = sigma * (1.0 + gate * (1.0 - sigma))
            terms = [scaled * up * slope, scaled * silu]
            terms.insert(2 * e, share * hidden)
            for k, term in enumerate(terms):
                left = (3 * e + k) * hs
                deltas[q, 0, :, left : left + hs] = term.astype(BF16)
            for one in ring[q][e][:2]:
                start(one)

    def token_terms(*qs):
        step = 1024
        into = [first_tg if q == 0 else dys.at[chunk_rows(q)] for q in qs]

        def body(n, carry):
            at_n = pl.ds(pl.multiple_of(n * step, step), step)
            both = dot(jnp.concatenate([deltas[one, 0, :, hs : 5 * hs] for one in qs], axis=0), wgu[at_n, :], 1, 1)
            for k, one in enumerate(into):
                one[:, at_n] = both[k * CHUNK : (k + 1) * CHUNK].astype(BF16)
            return carry

        lax.fori_loop(0, width // step, body, 0)

    def start_own_cols(q):
        for one in own_cols[q]:
            one.start()

    def pass_deltas(q):
        for e in range(EXPERTS):
            ring[q][e][e].wait_recv()
            start(ring[q][e][2])

    tile = 256
    drain = []

    def load_cols(q):
        bx.got_s(*chunk_slots[q])
        bd.got_s(*chunk_slots[q])
        if q == 0:
            for one in stage_own:
                one.wait()
        load[q].start()

    def weight_terms(q, first=False, last=False):
        for e in range(EXPERTS):
            ring[q][e][1 - e].wait_recv()
            ring[q][e][2].wait_recv()
        load[q].wait()
        mine = held.at[q % 2]
        rows = GROUPS * CHUNK
        delta = deltas.at[q]

        def one_tile(n):
            lanes = pl.ds(pl.multiple_of(n * tile, tile), tile)
            x = mine[0, :, :, lanes].reshape(rows, tile)
            return lanes, dot(x, delta[:, :, hs : 5 * hs].reshape(rows, 4 * hs), 0, 0)

        def body(n, carry):
            lanes, term = one_tile(n)
            if first:
                acc[lanes, :] = term
            else:
                acc[lanes, :] += term
            return carry

        if not last:
            lax.fori_loop(0, part // tile, body, 0)
        else:
            for n in range(part // tile):
                lanes, term = one_tile(n)
                total = (acc[n * tile : (n + 1) * tile, :] + term).astype(BF16)
                up_row, left = (n % 2) * tile, (n // 2) * 4 * hs
                xs[up_row : up_row + tile, left : left + 4 * hs] = total
                for e in range(EXPERTS):
                    for k, out in enumerate((gate_out, up_out)):
                        src = xs.at[
                            pl.ds(up_row, tile), pl.ds(left + (2 * e + k) * hs, hs)
                        ]
                        drain.append(local(src, out.at[e, pl.ds(n * tile, tile)]))
                        drain[-1].start()
        for e in range(EXPERTS):
            term = dot(
                delta[:, :, 5 * e * hs : (5 * e + 1) * hs].reshape(rows, hs),
                mine[1].reshape(rows, part), 0, 0,
            )
            if first:
                acc_down[e] = term
            elif not last:
                acc_down[e] += term
            else:
                left = 3 * 4 * hs
                xs[e * hs : (e + 1) * hs, left : left + part] = (acc_down[e] + term).astype(BF16)
                src = xs.at[pl.ds(e * hs, hs), pl.ds(left, part)]
                drain.append(local(src, down_out.at[e]))
                drain[-1].start()

    def token_rows(q, row, rows):
        if q == 0:
            return first_tg.at[pl.ds(row, rows)]
        return dys.at[pl.ds(q * CHUNK + row, rows)]

    pair = [
        copy(token_rows(q, other_row, CORE_ROWS), pair_in.at[q], sibling) for q in range(SIDE)
    ]
    lo, hi = pl.ds(0, half), pl.ds(half, half)

    def piece(q, u):
        return token_rows(q, core_row + u * PIECE, PIECE)

    def add(dst, lanes, *others):
        def body(n, carry):
            here = pl.ds(pl.multiple_of(n * LOCAL, LOCAL), LOCAL)
            total = dst[here, lanes].astype(F32)
            for one, cut in others:
                total += one[here, cut].astype(F32)
            dst[here, lanes] = total.astype(BF16)
            return carry

        lax.fori_loop(0, dst.shape[0] // LOCAL, body, 0)

    def pair_sum(q):
        pair[q].wait_recv()
        rows = token_rows(q, core_row, CORE_ROWS)
        add(rows, lo, (pair_in.at[q], lo))
        add(rows, hi, (pair_in.at[q], hi))

    whole = pl.ds(0, half)
    far_b = [
        (
            copy(piece(3, u).at[:, lo], half_b.at[u, 0], at(0, 1)),
            copy(piece(3, u).at[:, hi], half_b.at[u, 1], at(0, 3)),
        )
        for u in range(2)
    ]
    near_b = [
        (
            copy(piece(1 + u, 0).at[:, hi], half_b.at[u, 2], at(0, 1)),
            copy(piece(1 + u, 1).at[:, lo], half_b.at[u, 3], at(0, 3)),
            copy(piece(1 + u, 0).at[:, lo], half_b.at[u, 4], at(0, 1)),
            copy(piece(1 + u, 1).at[:, hi], half_b.at[u, 5], at(0, 3)),
        )
        for u in range(2)
    ]

    def far_to_near(u):
        far_b[u][0].wait_recv()
        add(piece(1 + u, 0), lo, (half_b.at[u, 0], whole))
        start(near_b[u][2])
        far_b[u][1].wait_recv()
        add(piece(1 + u, 1), hi, (half_b.at[u, 1], whole))
        start(near_b[u][3])

    def near_to_mine(u):
        for one in near_b[u]:
            one.wait_recv()
        add(piece(0, u), lo, (half_b.at[u, 3], whole), (half_b.at[u, 4], whole))
        add(piece(0, u), hi, (half_b.at[u, 2], whole), (half_b.at[u, 5], whole))

    def seat(i):
        return token_rows(0, slot_row(i, 0), LOCAL)

    far_a = (
        copy(seat(2).at[:, lo], half_a.at[0], at(1, 0)),
        copy(seat(2).at[:, hi], half_a.at[1], at(3, 0)),
    )
    near_a = (
        copy(seat(1).at[:, hi], half_a.at[2], at(1, 0)),
        copy(seat(3).at[:, lo], half_a.at[3], at(3, 0)),
        copy(seat(1).at[:, lo], half_a.at[4], at(1, 0)),
        copy(seat(3).at[:, hi], half_a.at[5], at(3, 0)),
    )

    to_c = copy(share_c.at[c], share_c.at[c], sibling)
    to_y = [copy(share_y.at[y], share_y.at[y], device(y + k, z, c)) for k in range(1, SIDE)]
    to_z = [copy(share_z.at[z], share_z.at[z], device(y, z + k, c)) for k in range(1, SIDE)]

    def prob_y():
        to_c.wait_recv()
        share_y[y] = share_c[0] + share_c[1]
        for one in to_y:
            start(one)

    def prob_z():
        for one in to_y:
            one.wait_recv()
        share_z[z] = (share_y[0] + share_y[1]) + (share_y[2] + share_y[3])
        for one in to_z:
            start(one)

    def prob_end():
        for one in to_z:
            one.wait_recv()
        prob_out[...] = (share_z[0] + share_z[1]) + (share_z[2] + share_z[3])

    def near_shards(x, d, u):
        for i in ORDER[2 * u : 2 * u + 2]:
            x.got_b(i, 3)
            d.got_b(i, 1)
            x.got_b(i, 1)
            d.got_b(i, 3)

    def far_shards(x, d):
        for i in ORDER:
            x.got_b(i, 2)
            d.got_b(i, 2)

    def first_shards(x, d):
        x.got_a(3)
        d.got_a(1)
        x.got_a(1)
        d.got_a(3)

    def token_part(*qs):
        for q in qs:
            if q > 0:
                sent(ad.from_chunk(q))
                for one in own_cols[q]:
                    one.wait()
        token_terms(*qs)
        for q in qs:
            start(pair[q])

    ax.begin_a()
    ad.begin_a()
    for one in fill:
        one.start()
    for one in swaps:
        start(one)
    share_c[c] = jnp.zeros(share_c.shape[1:], F32)
    ax.got_a(3)
    ax.begin_b()
    ad.begin_b()
    ad.got_a(1)
    ax.got_a(1)
    ad.got_a(3)
    ax.got_a(2)
    ad.got_a(2)
    for one in fill:
        one.wait()
    ax.got_s(*zero)
    ad.got_s(*zero)
    start_own_cols(0)
    forward(0)
    for one in swaps:
        one.wait_recv()
    for one in stage_own:
        one.start()

    near_shards(ax, ad, 0)
    bx.begin_a()
    bd.begin_a()
    ax.got_s(*near[0])
    ad.got_s(*near[0])
    start_own_cols(1)
    forward(1)
    pass_deltas(0)
    near_shards(ax, ad, 1)
    bx.begin_b()
    bd.begin_b()
    ax.got_s(*near[1])
    ad.got_s(*near[1])
    start_own_cols(2)
    forward(2)
    first_shards(bx, bd)
    token_part(0, 1)
    pass_deltas(1)
    far_shards(ax, ad)
    bx.got_a(2)
    bd.got_a(2)
    ax.got_s(*far)
    ad.got_s(*far)
    start_own_cols(3)
    forward(3)
    start(to_c)
    near_shards(bx, bd, 0)
    token_part(3, 2)
    pass_deltas(2)
    pair_sum(3)
    for u in range(2):
        start(far_b[u][0])
        start(far_b[u][1])
    near_shards(bx, bd, 1)
    pair_sum(1)
    start(near_b[0][0])
    start(near_b[0][1])
    pair_sum(2)
    start(near_b[1][0])
    start(near_b[1][1])
    prob_y()
    for one in own_cols[0]:
        one.wait()
    load_cols(0)
    load_cols(1)
    pass_deltas(3)
    weight_terms(0, first=True)
    far_to_near(0)
    far_to_near(1)
    prob_z()
    pair_sum(0)
    far_shards(bx, bd)
    load_cols(2)
    weight_terms(1)
    near_to_mine(0)
    near_to_mine(1)
    start(far_a[0])
    start(far_a[1])
    start(near_a[0])
    start(near_a[1])
    load_cols(3)
    prob_end()
    weight_terms(2)
    far_a[0].wait_recv()
    add(seat(1), lo, (half_a.at[0], whole))
    start(near_a[2])
    far_a[1].wait_recv()
    add(seat(3), hi, (half_a.at[1], whole))
    start(near_a[3])
    for q in range(SIDE):
        sent(ax.from_chunk(q))
    weight_terms(3, last=True)
    for one in near_a:
        one.wait_recv()
    mine = seat(0)[:, lo].astype(F32)
    mine += half_a[3].astype(F32)
    mine += half_a[4].astype(F32)
    token_out[:, lo] = mine.astype(BF16)
    mine = seat(0)[:, hi].astype(F32)
    mine += half_a[2].astype(F32)
    mine += half_a[5].astype(F32)
    token_out[:, hi] = mine.astype(BF16)
    sent(list(unsent))
    for one in drain:
        one.wait()


COPIES = 31 * 4 + 6 + 24 + 4 + 12 + 6 + 7
LOCALS = 7 + 12 + 2 + 26


def fused(tokens, out_grad, prob, w_gate, w_up, w_down):
    local, width = tokens.shape
    hs = w_gate.shape[2]
    part = width // GROUPS
    gtok = local * SLOTS
    anywhere = pl.BlockSpec(memory_space=pl.ANY)
    vmem = pl.BlockSpec(memory_space=pltpu.VMEM)
    flops = 2 * gtok * width * hs * 16
    return pl.pallas_call(
        kernel,
        out_shape=(
            jax.ShapeDtypeStruct((local, width), BF16),
            jax.ShapeDtypeStruct((SLOTS, 128), F32),
            jax.ShapeDtypeStruct((EXPERTS, part, hs), BF16),
            jax.ShapeDtypeStruct((EXPERTS, part, hs), BF16),
            jax.ShapeDtypeStruct((EXPERTS, hs, part), BF16),
            jax.ShapeDtypeStruct((2, SIDE, GROUPS, CHUNK, part), BF16),
        ),
        in_specs=[anywhere, anywhere, vmem, anywhere, anywhere, anywhere],
        out_specs=(vmem, vmem, anywhere, anywhere, anywhere, anywhere),
        scratch_shapes=[
            pltpu.VMEM((gtok, width), BF16),
            pltpu.VMEM((gtok, width), BF16),
            pltpu.VMEM((width, 4 * hs), BF16),
            pltpu.VMEM(w_down.shape, BF16),
            pltpu.VMEM((SIDE, GROUPS, CHUNK, 6 * hs), BF16),
            pltpu.VMEM((SIDE, CORE_ROWS, width), BF16),
            pltpu.VMEM((2, 6, PIECE, width // 2), BF16),
            pltpu.VMEM((6, LOCAL, width // 2), BF16),
            pltpu.VMEM((2, GROUPS - 1, LOCAL, part), BF16),
            pltpu.VMEM((2, 2, GROUPS, CHUNK, part), BF16),
            pltpu.VMEM((CHUNK, width), BF16),
            pltpu.VMEM((part, 4 * hs), F32),
            pltpu.VMEM((EXPERTS, hs, part), F32),
            pltpu.VMEM((2, SLOTS, 128), F32),
            pltpu.VMEM((SIDE, SLOTS, 128), F32),
            pltpu.VMEM((SIDE, SLOTS, 128), F32),
            pltpu.SemaphoreType.DMA((LOCALS,)),
            pltpu.SemaphoreType.DMA((COPIES,)),
            pltpu.SemaphoreType.DMA((COPIES,)),
        ],
        compiler_params=pltpu.CompilerParams(
            collective_id=0, has_side_effects=True, vmem_limit_bytes=62 << 20
        ),
        cost_estimate=pl.CostEstimate(flops=flops, bytes_accessed=60 << 20, transcendentals=0),
    )(tokens, out_grad, prob, w_gate, w_up, w_down)


def shards(tokens, out_grad, row_prob, row_token, block_expert, w_gate, w_up, w_down):
    local, width = tokens.shape[1:]
    gtok = local * SLOTS
    row_expert = jnp.repeat(block_expert[0], BLOCK)
    token = row_token[0]

    y, z, c = place()
    source = token // LOCAL
    off_y = (source // (2 * SIDE) - y) % SIDE
    off_z = ((source // 2) % SIDE - z) % SIDE
    core = source % 2
    i = jnp.where(core == 0, off_y, off_z)
    j = jnp.where(core == 0, off_z, off_y)
    seat = jnp.where(i == 0, 0, jnp.where(i == 3, 1, i + 1))
    near = (1 + seat // 2) * CHUNK + (j // 2) * PIECE + (seat % 2) * LOCAL
    row = jnp.where(j % 2 == 1, near, (j // 2) * 3 * CHUNK + seat * LOCAL)
    row = jnp.where(token < gtok, row + core * CORE_ROWS + token % LOCAL, gtok)
    every = jnp.arange(gtok, dtype=jnp.int32)[None, :]
    hit = row[:, None] == every
    prob = jnp.stack(
        [
            jnp.sum(jnp.where(hit & (row_expert == e)[:, None], row_prob[0][:, None], 0.0), axis=0)
            for e in range(EXPERTS)
        ],
        axis=1,
    )
    token_sum, prob_total, gate_grad, up_grad, down_grad, _ = fused(
        tokens[0], out_grad[0], prob, w_gate, w_up, w_down
    )
    prob_tok = [prob_total[:, e * LOCAL : (e + 1) * LOCAL].reshape(gtok) for e in range(EXPERTS)]
    mine = jnp.where((row_expert == 0)[:, None], prob_tok[0][None], prob_tok[1][None])
    prob_sum = jnp.sum(jnp.where(token[:, None] == every, mine, 0.0), axis=1)
    return (token_sum[None], prob_sum[None], gate_grad, up_grad, down_grad)


def solution(mesh):
    in_specs = (
        P("dp", "fsdp", None),
        P("dp", "fsdp", None),
        P("dp", None),
        P("dp", None),
        P("dp", None),
        P(None, None, "fsdp"),
        P(None, None, "fsdp"),
        P(None, "fsdp", None),
    )
    out_specs = (
        P("dp", "fsdp", None),
        P("dp", None),
        P(None, "dp", "fsdp"),
        P(None, "dp", "fsdp"),
        P(None, "fsdp", "dp"),
    )
    return jax.shard_map(shards, mesh=mesh, in_specs=in_specs, out_specs=out_specs, check_vma=False)
```

```python
import functools

import jax
import jax.numpy as jnp
from jax import lax
from jax.experimental import pallas as pl
from jax.experimental.pallas import tpu as pltpu
from jax.sharding import PartitionSpec as P

EXPERTS = 2
BLOCK = 128
SIDE = 4
GROUPS = 4
LOCAL = 16
SLOTS = 32
CHUNK = 128
CORE_ROWS = CHUNK // 2
PIECE = CORE_ROWS // 2
ORDER = (0, 3, 1, 2)
SEAT = (0, 2, 3, 1)
BF16 = jnp.bfloat16
F32 = jnp.float32


def dot(a, b, ca, cb):
    return lax.dot_general(a, b, (((ca,), (cb,)), ((), ())), preferred_element_type=F32)


def offset_row(i, j):
    seat = SEAT[i]
    if j == 0:
        return seat * LOCAL
    if j == 2:
        return 3 * CHUNK + seat * LOCAL
    return (1 + seat // 2) * CHUNK + (j // 2) * PIECE + (seat % 2) * LOCAL


def place():
    f = lax.axis_index("fsdp")
    return f // (2 * SIDE), (f // 2) % SIDE, f % 2


def kernel(
    tokens, out_grad, prob, w_gate, w_up, w_down,
    token_out, prob_out, gate_out, up_out, down_out, cols,
    xs, dys, wgu, wd, deltas, pair_in, half_b, half_a, stage, held, first_tg, acc, acc_down,
    share_c, share_y, share_z, local_sem, send, recv,
):
    y, z, c = place()
    p = lax.axis_index("dp")
    width = xs.shape[1]
    half = width // 2
    part = width // GROUPS
    hs = wd.shape[1]
    count = [0]
    locals_ = [0]

    def device(yy, zz, cc):
        return {"fsdp": ((yy % SIDE) * SIDE + zz % SIDE) * 2 + cc}

    def at(da, db):
        return device(y + (1 - c) * da + c * db, z + c * da + (1 - c) * db, c)

    sibling = device(y, z, 1 - c)

    def over(k):
        return {"dp": (p + k) % GROUPS}

    barrier = pltpu.get_barrier_semaphore()
    peers = [at(1, 0), at(2, 0), at(3, 0), at(0, 1), at(0, 2), at(0, 3), sibling]
    peers += [over(1), over(2), over(3)]
    for peer in peers:
        pl.semaphore_signal(barrier, inc=1, device_id=peer, device_id_type=pl.DeviceIdType.MESH)
    pl.semaphore_wait(barrier, len(peers))

    unsent = []

    def copy(src, dst, to):
        n = count[0]
        count[0] += 1
        return pltpu.make_async_remote_copy(
            src_ref=src, dst_ref=dst, send_sem=send.at[n], recv_sem=recv.at[n],
            device_id=to, device_id_type=pl.DeviceIdType.MESH,
        )

    def local(src, dst):
        n = locals_[0]
        locals_[0] += 1
        return pltpu.make_async_copy(src, dst, local_sem.at[n])

    def start(one):
        one.start()
        unsent.append(one)

    def sent(ones):
        for one in ones:
            one.wait_send()
            unsent[:] = [copied for copied in unsent if copied is not one]

    core_row = pl.multiple_of(c * CORE_ROWS, CORE_ROWS)
    other_row = pl.multiple_of((1 - c) * CORE_ROWS, CORE_ROWS)

    def slot_row(i, j):
        return pl.multiple_of(core_row + offset_row(i, j), LOCAL)

    class Gather:
        def __init__(self, slot, mine, plus):
            far = 3 if plus else 1
            self.plus, self.far = plus, far
            self.a = {3: copy(mine, slot(3, 0), at(1, 0)), 1: copy(mine, slot(1, 0), at(3, 0))}
            self.a[2] = copy(slot(far, 0), slot(2, 0), at(1 if plus else 3, 0))
            self.b, self.s = {}, {}
            for i in range(SIDE):
                src = mine if i == 0 else slot(i, 0)
                self.b[i, 3] = copy(src, slot(i, 3), at(0, 1))
                self.b[i, 1] = copy(src, slot(i, 1), at(0, 3))
                self.b[i, 2] = copy(slot(i, far), slot(i, 2), at(0, 1 if plus else 3))
                for j in range(SIDE):
                    src = mine if i == 0 and j == 0 else slot(i, j)
                    self.s[i, j] = copy(src, slot(i, j), sibling)

        def begin_a(self):
            start(self.a[3])
            start(self.a[1])

        def begin_b(self):
            start(self.b[0, 3])
            start(self.b[0, 1])
            start(self.s[0, 0])

        def got_a(self, i):
            self.a[i].wait_recv()
            if i == self.far:
                start(self.a[2])
            start(self.b[i, 3])
            start(self.b[i, 1])
            start(self.s[i, 0])

        def got_b(self, i, j):
            self.b[i, j].wait_recv()
            if j == self.far:
                start(self.b[i, 2])
            start(self.s[i, j])

        def got_s(self, *slots):
            for slot in slots:
                self.s[slot].wait_recv()

        def from_chunk(self, q):
            if q == 0:
                ones = [self.a[2]] + [self.b[i, j] for i in (1, 2, 3) for j in (1, 3)]
                return ones + [self.s[i, 0] for i in (1, 2, 3)]
            if q == 3:
                return [self.s[i, 2] for i in range(SIDE)]
            ones = []
            for i in ORDER[2 * q - 2 : 2 * q]:
                ones += [self.b[i, 2], self.s[i, 1], self.s[i, 3]]
            return ones

    zero = [(i, 0) for i in range(SIDE)]
    near = [[(i, j) for i in ORDER[2 * u : 2 * u + 2] for j in (1, 3)] for u in range(2)]
    far = [(i, 2) for i in range(SIDE)]
    chunk_slots = [zero, near[0], near[1], far]

    def chunk_rows(q):
        return pl.ds(q * CHUNK, CHUNK)

    row0 = slot_row(0, 0)
    fill = [
        local(tokens, xs.at[pl.ds(row0, LOCAL)]),
        local(out_grad, dys.at[pl.ds(row0, LOCAL)]),
        local(w_gate.at[0], wgu.at[:, pl.ds(0, hs)]),
        local(w_up.at[0], wgu.at[:, pl.ds(hs, hs)]),
        local(w_down, wd),
        local(w_gate.at[1], wgu.at[:, pl.ds(2 * hs, hs)]),
        local(w_up.at[1], wgu.at[:, pl.ds(3 * hs, hs)]),
    ]
    ax = Gather(lambda i, j: xs.at[pl.ds(slot_row(i, j), LOCAL)], tokens, True)
    ad = Gather(lambda i, j: dys.at[pl.ds(slot_row(i, j), LOCAL)], out_grad, False)

    def col_slot(k):
        def slot(i, j):
            row = offset_row(i, j)
            rows = pl.ds(pl.multiple_of(core_row + row % CHUNK, LOCAL), LOCAL)
            return cols.at[k, row // CHUNK, pl.ds(1, GROUPS - 1), rows]

        return slot

    bx = Gather(col_slot(0), stage.at[0], True)
    bd = Gather(col_slot(1), stage.at[1], False)
    swaps = []
    for k, src in enumerate((tokens, out_grad)):
        for step in range(1, GROUPS):
            lane = pl.multiple_of(((p + step) % GROUPS) * part, part)
            swaps.append(
                copy(src.at[:, pl.ds(lane, part)], stage.at[k, GROUPS - step - 1], over(step))
            )

    ring, own_cols, load = {}, {}, {}
    lane = pl.multiple_of(p * part, part)
    for q in range(SIDE):
        ring[q] = []
        for e in range(EXPERTS):
            cut = pl.ds(3 * e * hs, 3 * hs)
            here = deltas.at[q, 0, :, cut]
            passed = deltas.at[q, (3, 1)[e], :, cut]
            ring[q].append(
                (
                    copy(here, deltas.at[q, 3, :, cut], over(1)),
                    copy(here, deltas.at[q, 1, :, cut], over(3)),
                    copy(passed, deltas.at[q, 2, :, cut], over((1, 3)[e])),
                )
            )
        own_cols[q] = (
            local(xs.at[chunk_rows(q), pl.ds(lane, part)], cols.at[0, q, 0]),
            local(dys.at[chunk_rows(q), pl.ds(lane, part)], cols.at[1, q, 0]),
        )
        load[q] = local(cols.at[:, q], held.at[q % 2])
    stage_own = [local(stage.at[k], col_slot(k)(0, 0)) for k in range(2)]

    def forward(q):
        where = chunk_rows(q)
        for e in range(EXPERTS):
            gate_up = dot(xs[where], wgu[:, 2 * e * hs : (2 * e + 2) * hs], 1, 0)
            gate, up = gate_up[:, :hs], gate_up[:, hs:]
            back = dot(dys[where], wd[e], 1, 1)
            sigma = jax.nn.sigmoid(gate)
            silu = gate * sigma
            hidden = (silu * up).astype(BF16).astype(F32)
            product = hidden * back
            folded = product[:, : hs // 2] + product[:, hs // 2 :]
            row = jnp.sum(jnp.transpose(folded), axis=0, keepdims=True)
            for k in range(2):
                for i, j in chunk_slots[q]:
                    first = k * CORE_ROWS + offset_row(i, j) % CHUNK
                    owner = device(y + (1 - k) * i + k * j, z + k * i + (1 - k) * j, k)["fsdp"]
                    share_c[c, pl.ds(owner, 1), e * LOCAL : (e + 1) * LOCAL] = row[
                        :, first : first + LOCAL
                    ]
            shares = jnp.broadcast_to(prob[e : e + 1, where], (CHUNK, CHUNK))
            share = jnp.transpose(shares)[:, :1]
            scaled = share * back
            slope = sigma * (1.0 + gate * (1.0 - sigma))
            terms = [scaled * up * slope, scaled * silu]
            terms.insert(2 * e, share * hidden)
            for k, term in enumerate(terms):
                left = (3 * e + k) * hs
                deltas[q, 0, :, left : left + hs] = term.astype(BF16)
            for one in ring[q][e][:2]:
                start(one)

    def token_terms(*qs):
        step = 1024
        into = [first_tg if q == 0 else dys.at[chunk_rows(q)] for q in qs]

        def body(n, carry):
            at_n = pl.ds(pl.multiple_of(n * step, step), step)
            both = dot(jnp.concatenate([deltas[one, 0, :, hs : 5 * hs] for one in qs], axis=0), wgu[at_n, :], 1, 1)
            for k, one in enumerate(into):
                one[:, at_n] = both[k * CHUNK : (k + 1) * CHUNK].astype(BF16)
            return carry

        lax.fori_loop(0, width // step, body, 0)

    def start_own_cols(q):
        for one in own_cols[q]:
            one.start()

    def pass_deltas(q):
        for e in range(EXPERTS):
            ring[q][e][e].wait_recv()
            start(ring[q][e][2])

    tile = 256
    drain = []

    def load_cols(q):
        bx.got_s(*chunk_slots[q])
        bd.got_s(*chunk_slots[q])
        if q == 0:
            for one in stage_own:
                one.wait()
        load[q].start()

    def weight_terms(q, first=False, last=False):
        for e in range(EXPERTS):
            ring[q][e][1 - e].wait_recv()
            ring[q][e][2].wait_recv()
        load[q].wait()
        mine = held.at[q % 2]
        rows = GROUPS * CHUNK
        delta = deltas.at[q]

        def one_tile(n):
            lanes = pl.ds(pl.multiple_of(n * tile, tile), tile)
            x = mine[0, :, :, lanes].reshape(rows, tile)
            return lanes, dot(x, delta[:, :, hs : 5 * hs].reshape(rows, 4 * hs), 0, 0)

        def body(n, carry):
            lanes, term = one_tile(n)
            if first:
                acc[lanes, :] = term
            else:
                acc[lanes, :] += term
            return carry

        if not last:
            lax.fori_loop(0, part // tile, body, 0)
        else:
            for n in range(part // tile):
                lanes, term = one_tile(n)
                total = (acc[n * tile : (n + 1) * tile, :] + term).astype(BF16)
                up_row, left = (n % 2) * tile, (n // 2) * 4 * hs
                xs[up_row : up_row + tile, left : left + 4 * hs] = total
                for e in range(EXPERTS):
                    for k, out in enumerate((gate_out, up_out)):
                        src = xs.at[
                            pl.ds(up_row, tile), pl.ds(left + (2 * e + k) * hs, hs)
                        ]
                        drain.append(local(src, out.at[e, pl.ds(n * tile, tile)]))
                        drain[-1].start()
        for e in range(EXPERTS):
            term = dot(
                delta[:, :, 5 * e * hs : (5 * e + 1) * hs].reshape(rows, hs),
                mine[1].reshape(rows, part), 0, 0,
            )
            if first:
                acc_down[e] = term
            elif not last:
                acc_down[e] += term
            else:
                left = 3 * 4 * hs
                xs[e * hs : (e + 1) * hs, left : left + part] = (acc_down[e] + term).astype(BF16)
                src = xs.at[pl.ds(e * hs, hs), pl.ds(left, part)]
                drain.append(local(src, down_out.at[e]))
                drain[-1].start()

    def token_rows(q, row, rows):
        if q == 0:
            return first_tg.at[pl.ds(row, rows)]
        return dys.at[pl.ds(q * CHUNK + row, rows)]

    pair = [
        copy(token_rows(q, other_row, CORE_ROWS), pair_in.at[q], sibling) for q in range(SIDE)
    ]
    lo, hi = pl.ds(0, half), pl.ds(half, half)

    def piece(q, u):
        return token_rows(q, core_row + u * PIECE, PIECE)

    def add(dst, lanes, *others):
        def body(n, carry):
            here = pl.ds(pl.multiple_of(n * LOCAL, LOCAL), LOCAL)
            total = dst[here, lanes].astype(F32)
            for one, cut in others:
                total += one[here, cut].astype(F32)
            dst[here, lanes] = total.astype(BF16)
            return carry

        lax.fori_loop(0, dst.shape[0] // LOCAL, body, 0)

    def pair_sum(q):
        pair[q].wait_recv()
        rows = token_rows(q, core_row, CORE_ROWS)
        add(rows, lo, (pair_in.at[q], lo))
        add(rows, hi, (pair_in.at[q], hi))

    whole = pl.ds(0, half)
    far_b = [
        (
            copy(piece(3, u).at[:, lo], half_b.at[u, 0], at(0, 1)),
            copy(piece(3, u).at[:, hi], half_b.at[u, 1], at(0, 3)),
        )
        for u in range(2)
    ]
    near_b = [
        (
            copy(piece(1 + u, 0).at[:, hi], half_b.at[u, 2], at(0, 1)),
            copy(piece(1 + u, 1).at[:, lo], half_b.at[u, 3], at(0, 3)),
            copy(piece(1 + u, 0).at[:, lo], half_b.at[u, 4], at(0, 1)),
            copy(piece(1 + u, 1).at[:, hi], half_b.at[u, 5], at(0, 3)),
        )
        for u in range(2)
    ]

    def far_to_near(u):
        far_b[u][0].wait_recv()
        add(piece(1 + u, 0), lo, (half_b.at[u, 0], whole))
        start(near_b[u][2])
        far_b[u][1].wait_recv()
        add(piece(1 + u, 1), hi, (half_b.at[u, 1], whole))
        start(near_b[u][3])

    def near_to_mine(u):
        for one in near_b[u]:
            one.wait_recv()
        add(piece(0, u), lo, (half_b.at[u, 3], whole), (half_b.at[u, 4], whole))
        add(piece(0, u), hi, (half_b.at[u, 2], whole), (half_b.at[u, 5], whole))

    def seat(i):
        return token_rows(0, slot_row(i, 0), LOCAL)

    far_a = (
        copy(seat(2).at[:, lo], half_a.at[0], at(1, 0)),
        copy(seat(2).at[:, hi], half_a.at[1], at(3, 0)),
    )
    near_a = (
        copy(seat(1).at[:, hi], half_a.at[2], at(1, 0)),
        copy(seat(3).at[:, lo], half_a.at[3], at(3, 0)),
        copy(seat(1).at[:, lo], half_a.at[4], at(1, 0)),
        copy(seat(3).at[:, hi], half_a.at[5], at(3, 0)),
    )

    to_c = copy(share_c.at[c], share_c.at[c], sibling)
    to_y = [copy(share_y.at[y], share_y.at[y], device(y + k, z, c)) for k in range(1, SIDE)]
    to_z = [copy(share_z.at[z], share_z.at[z], device(y, z + k, c)) for k in range(1, SIDE)]

    def prob_y():
        to_c.wait_recv()
        share_y[y] = share_c[0] + share_c[1]
        for one in to_y:
            start(one)

    def prob_z():
        for one in to_y:
            one.wait_recv()
        share_z[z] = (share_y[0] + share_y[1]) + (share_y[2] + share_y[3])
        for one in to_z:
            start(one)

    def prob_end():
        for one in to_z:
            one.wait_recv()
        prob_out[...] = (share_z[0] + share_z[1]) + (share_z[2] + share_z[3])

    def near_shards(x, d, u):
        for i in ORDER[2 * u : 2 * u + 2]:
            x.got_b(i, 3)
            d.got_b(i, 1)
            x.got_b(i, 1)
            d.got_b(i, 3)

    def far_shards(x, d):
        for i in ORDER:
            x.got_b(i, 2)
            d.got_b(i, 2)

    def first_shards(x, d):
        x.got_a(3)
        d.got_a(1)
        x.got_a(1)
        d.got_a(3)

    def token_part(*qs):
        for q in qs:
            if q > 0:
                sent(ad.from_chunk(q))
                for one in own_cols[q]:
                    one.wait()
        token_terms(*qs)
        for q in qs:
            start(pair[q])

    ax.begin_a()
    ad.begin_a()
    for one in fill:
        one.start()
    for one in swaps:
        start(one)
    share_c[c] = jnp.zeros(share_c.shape[1:], F32)
    ax.got_a(3)
    ax.begin_b()
    ad.begin_b()
    ad.got_a(1)
    ax.got_a(1)
    ad.got_a(3)
    ax.got_a(2)
    ad.got_a(2)
    for one in fill:
        one.wait()
    ax.got_s(*zero)
    ad.got_s(*zero)
    start_own_cols(0)
    forward(0)
    for one in swaps:
        one.wait_recv()
    for one in stage_own:
        one.start()

    bx.begin_a()
    bd.begin_a()
    bx.begin_b()
    bd.begin_b()
    near_shards(ax, ad, 0)
    ax.got_s(*near[0])
    ad.got_s(*near[0])
    start_own_cols(1)
    forward(1)
    pass_deltas(0)
    near_shards(ax, ad, 1)
    ax.got_s(*near[1])
    ad.got_s(*near[1])
    start_own_cols(2)
    forward(2)
    first_shards(bx, bd)
    token_part(0, 1)
    pass_deltas(1)
    far_shards(ax, ad)
    bx.got_a(2)
    bd.got_a(2)
    ax.got_s(*far)
    ad.got_s(*far)
    start_own_cols(3)
    forward(3)
    start(to_c)
    near_shards(bx, bd, 0)
    token_part(3, 2)
    pass_deltas(2)
    pair_sum(3)
    for u in range(2):
        start(far_b[u][0])
        start(far_b[u][1])
    near_shards(bx, bd, 1)
    pair_sum(1)
    start(near_b[0][0])
    start(near_b[0][1])
    pair_sum(2)
    start(near_b[1][0])
    start(near_b[1][1])
    prob_y()
    for one in own_cols[0]:
        one.wait()
    load_cols(0)
    load_cols(1)
    pass_deltas(3)
    weight_terms(0, first=True)
    far_to_near(0)
    far_to_near(1)
    prob_z()
    pair_sum(0)
    far_shards(bx, bd)
    load_cols(2)
    weight_terms(1)
    near_to_mine(0)
    near_to_mine(1)
    start(far_a[0])
    start(far_a[1])
    start(near_a[0])
    start(near_a[1])
    load_cols(3)
    prob_end()
    weight_terms(2)
    far_a[0].wait_recv()
    add(seat(1), lo, (half_a.at[0], whole))
    start(near_a[2])
    far_a[1].wait_recv()
    add(seat(3), hi, (half_a.at[1], whole))
    start(near_a[3])
    for q in range(SIDE):
        sent(ax.from_chunk(q))
    weight_terms(3, last=True)
    for one in near_a:
        one.wait_recv()
    mine = seat(0)[:, lo].astype(F32)
    mine += half_a[3].astype(F32)
    mine += half_a[4].astype(F32)
    token_out[:, lo] = mine.astype(BF16)
    mine = seat(0)[:, hi].astype(F32)
    mine += half_a[2].astype(F32)
    mine += half_a[5].astype(F32)
    token_out[:, hi] = mine.astype(BF16)
    sent(list(unsent))
    for one in drain:
        one.wait()


COPIES = 31 * 4 + 6 + 24 + 4 + 12 + 6 + 7
LOCALS = 7 + 12 + 2 + 26


def fused(tokens, out_grad, prob, w_gate, w_up, w_down):
    local, width = tokens.shape
    hs = w_gate.shape[2]
    part = width // GROUPS
    gtok = local * SLOTS
    anywhere = pl.BlockSpec(memory_space=pl.ANY)
    vmem = pl.BlockSpec(memory_space=pltpu.VMEM)
    flops = 2 * gtok * width * hs * 16
    return pl.pallas_call(
        kernel,
        out_shape=(
            jax.ShapeDtypeStruct((local, width), BF16),
            jax.ShapeDtypeStruct((SLOTS, 128), F32),
            jax.ShapeDtypeStruct((EXPERTS, part, hs), BF16),
            jax.ShapeDtypeStruct((EXPERTS, part, hs), BF16),
            jax.ShapeDtypeStruct((EXPERTS, hs, part), BF16),
            jax.ShapeDtypeStruct((2, SIDE, GROUPS, CHUNK, part), BF16),
        ),
        in_specs=[anywhere, anywhere, vmem, anywhere, anywhere, anywhere],
        out_specs=(vmem, vmem, anywhere, anywhere, anywhere, anywhere),
        scratch_shapes=[
            pltpu.VMEM((gtok, width), BF16),
            pltpu.VMEM((gtok, width), BF16),
            pltpu.VMEM((width, 4 * hs), BF16),
            pltpu.VMEM(w_down.shape, BF16),
            pltpu.VMEM((SIDE, GROUPS, CHUNK, 6 * hs), BF16),
            pltpu.VMEM((SIDE, CORE_ROWS, width), BF16),
            pltpu.VMEM((2, 6, PIECE, width // 2), BF16),
            pltpu.VMEM((6, LOCAL, width // 2), BF16),
            pltpu.VMEM((2, GROUPS - 1, LOCAL, part), BF16),
            pltpu.VMEM((2, 2, GROUPS, CHUNK, part), BF16),
            pltpu.VMEM((CHUNK, width), BF16),
            pltpu.VMEM((part, 4 * hs), F32),
            pltpu.VMEM((EXPERTS, hs, part), F32),
            pltpu.VMEM((2, SLOTS, 128), F32),
            pltpu.VMEM((SIDE, SLOTS, 128), F32),
            pltpu.VMEM((SIDE, SLOTS, 128), F32),
            pltpu.SemaphoreType.DMA((LOCALS,)),
            pltpu.SemaphoreType.DMA((COPIES,)),
            pltpu.SemaphoreType.DMA((COPIES,)),
        ],
        compiler_params=pltpu.CompilerParams(
            collective_id=0, has_side_effects=True, vmem_limit_bytes=62 << 20
        ),
        cost_estimate=pl.CostEstimate(flops=flops, bytes_accessed=60 << 20, transcendentals=0),
    )(tokens, out_grad, prob, w_gate, w_up, w_down)


def shards(tokens, out_grad, row_prob, row_token, block_expert, w_gate, w_up, w_down):
    local, width = tokens.shape[1:]
    gtok = local * SLOTS
    row_expert = jnp.repeat(block_expert[0], BLOCK)
    token = row_token[0]

    y, z, c = place()
    source = token // LOCAL
    off_y = (source // (2 * SIDE) - y) % SIDE
    off_z = ((source // 2) % SIDE - z) % SIDE
    core = source % 2
    i = jnp.where(core == 0, off_y, off_z)
    j = jnp.where(core == 0, off_z, off_y)
    seat = jnp.where(i == 0, 0, jnp.where(i == 3, 1, i + 1))
    near = (1 + seat // 2) * CHUNK + (j // 2) * PIECE + (seat % 2) * LOCAL
    row = jnp.where(j % 2 == 1, near, (j // 2) * 3 * CHUNK + seat * LOCAL)
    row = jnp.where(token < gtok, row + core * CORE_ROWS + token % LOCAL, gtok)
    every = jnp.arange(gtok, dtype=jnp.int32)[None, :]
    hit = row[:, None] == every
    prob = jnp.stack(
        [
            jnp.sum(jnp.where(hit & (row_expert == e)[:, None], row_prob[0][:, None], 0.0), axis=0)
            for e in range(EXPERTS)
        ]
    )
    token_sum, prob_total, gate_grad, up_grad, down_grad, _ = fused(
        tokens[0], out_grad[0], prob, w_gate, w_up, w_down
    )
    prob_tok = [prob_total[:, e * LOCAL : (e + 1) * LOCAL].reshape(gtok) for e in range(EXPERTS)]
    mine = jnp.where((row_expert == 0)[:, None], prob_tok[0][None], prob_tok[1][None])
    prob_sum = jnp.sum(jnp.where(token[:, None] == every, mine, 0.0), axis=1)
    return (token_sum[None], prob_sum[None], gate_grad, up_grad, down_grad)


def solution(mesh):
    in_specs = (
        P("dp", "fsdp", None),
        P("dp", "fsdp", None),
        P("dp", None),
        P("dp", None),
        P("dp", None),
        P(None, None, "fsdp"),
        P(None, None, "fsdp"),
        P(None, "fsdp", None),
    )
    out_specs = (
        P("dp", "fsdp", None),
        P("dp", None),
        P(None, "dp", "fsdp"),
        P(None, "dp", "fsdp"),
        P(None, "fsdp", "dp"),
    )
    return jax.shard_map(shards, mesh=mesh, in_specs=in_specs, out_specs=out_specs, check_vma=False)
```
